32 devices in a mesh: groups: 2 (over y), nodes: 4 (over z), feat: 2 (over x), chan: 2 (over core).
Axes of the slice: x: 2, y: 2, z: 4, core: 2. Of those that a mesh axis runs over, the one named last changes fastest.
Arguments:
- node_latents: bfloat16 [3072, 512], P(('groups', 'nodes'), 'chan'), parts along dimension 0, may hold values from -6 to 6
- edge_latents: bfloat16 [24576, 512], P(('groups', 'nodes'), 'chan'), parts along dimension 0, may hold values from -6 to 6
- sender_latents: bfloat16 [24576, 512], P(('groups', 'nodes'), 'chan'), parts along dimension 0, may hold values from -6 to 6
- pre_hidden: bfloat16 [24576, 512], P(('groups', 'nodes'), 'feat'), parts along dimension 0, may hold values from -6 to 6
- pre_norm: bfloat16 [24576, 512], P(('groups', 'nodes'), 'chan'), parts along dimension 0, may hold values from -300 to 300
- norm_gain: float32 [512], P('chan'), may hold values from 0.5 to 1.5
- w_in: bfloat16 [3, 512, 512], P(None, 'chan'), may hold values from -0.15625 to 0.15625
- w_out: bfloat16 [512, 512], P('feat', 'chan'), may hold values from -0.25 to 0.25
- senders: int32 [24576], P(('groups', 'nodes')), parts along dimension 0, may hold values from 0 to 1535, as said below
- receivers: int32 [24576], P(('groups', 'nodes')), parts along dimension 0, may hold values from 0 to 1535, as said below
- edge_cotangent: bfloat16 [24576, 512], P(('groups', 'nodes'), 'chan'), parts along dimension 0, may hold values from -6 to 6
- agg_cotangent: bfloat16 [3072, 512], P(('groups', 'nodes'), 'chan'), parts along dimension 0, may hold values from -6 to 6
Outputs:
- node_grad: float32 [3072, 512], P(('groups', 'nodes'), 'chan'), parts along dimension 0
- edge_grad: bfloat16 [24576, 512], P(('groups', 'nodes'), 'chan'), parts along dimension 0
- w_in_grad: float32 [6, 512, 512], P('groups', 'chan', 'feat'), parts along dimension 0
- w_out_grad: float32 [1024, 512], P(('groups', 'feat'), 'chan'), parts along dimension 0
- gain_grad: float32 [1024], P(('groups', 'chan')), parts along dimension 0
The draws below stay inside these ranges and needn't reach their ends.
There are 2 independent parts, one for each index of `groups`. The reference program is written for one: setup_inputs(seed, part) draws one part's arguments, and reference() takes and returns one part's arrays. A program takes and returns all parts, laid end to end along the dimension named above; an argument that names none is the same for every part. Nothing has to cross between parts.
Inputs may be any that keep to these rules, and one draw needn't show every extreme that they name: Of the 3072 edges of one index of nodes (edges 3072 * i to 3072 * i + 3071, whose nodes are 384 * i to 384 * i + 383), exactly 1536 have senders on other indices, and at most 1024 on any one other index; some index receives exactly 1024 from every other index. `receivers`: each edge's receiver lies among the 384 nodes of the index of nodes that holds the edge.
All inputs are finite; a program needn't handle non-finite values.
Results may differ from the reference program's by a relative error of at most 0.0055.
Values may be sent and summed in bfloat16 or wider, within the bound.
No kernel may reach another device: no remote copies, remote signals or barrier semaphores. Data moves between devices by JAX's collectives and lax.ppermute only.
A program may use at most 128 MiB of HBM per device.

```python
import math
import jax
import jax.numpy as jnp
from jax import lax

D = 512
H = 512
NODE_DEV = 384
EDGE_DEV = 3072
NODES = 1536
EDGES = 12288


def draw_senders(key, part):
    key = jax.random.fold_in(key, 11)
    shards = NODES // NODE_DEV
    remote = EDGE_DEV // 2
    capacity = (EDGE_DEV + shards - 2) // (shards - 1)
    key_target, key_rest = jax.random.split(key)
    target = jax.random.randint(key_target, (), 0, shards, dtype=jnp.int32)
    shard_keys = jax.random.split(key_rest, shards)

    def per_shard(shard_key, shard):
        key_other, key_slots, key_nodes, key_order = jax.random.split(shard_key, 4)
        other_shard = (target + 1 + jax.random.randint(key_other, (), 0, shards - 1, dtype=jnp.int32)) % shards
        full_shard = jnp.where(shard == target, other_shard, target)
        slot_ids = jax.random.permutation(key_slots, (shards - 2) * capacity)[:remote - capacity].astype(jnp.int32)
        picked = slot_ids // capacity
        low_skip = jnp.minimum(shard, full_shard)
        high_skip = jnp.maximum(shard, full_shard)
        shifted = picked + (picked >= low_skip).astype(jnp.int32)
        shifted = shifted + (shifted >= high_skip).astype(jnp.int32)
        destination = jnp.concatenate([jnp.full((capacity,), 1, jnp.int32) * full_shard, shifted, jnp.full((EDGE_DEV - remote,), 1, jnp.int32) * shard])
        node_ids = jax.random.randint(key_nodes, (EDGE_DEV,), 0, NODE_DEV, dtype=jnp.int32)
        global_ids = destination * NODE_DEV + node_ids
        shuffle = jax.random.permutation(key_order, EDGE_DEV)
        return global_ids[shuffle]
    result = jax.vmap(per_shard)(shard_keys, jnp.arange(shards, dtype=jnp.int32))
    return result.reshape(-1).astype(jnp.int32)


def draw_receivers(key, part):
    key = jax.random.fold_in(key, 12)
    first_node = jnp.arange(EDGES, dtype=jnp.int32) // EDGE_DEV * NODE_DEV
    return (first_node + jax.random.randint(key, (EDGES,), 0, NODE_DEV, dtype=jnp.int32)).astype(jnp.int32)


def draw_pre_norm(key, part):
    key = jax.random.fold_in(key, 13)
    key_rows, key_cols, key_shift, key_base = jax.random.split(key, 4)
    ramp = 1.0 + 2.0 * jnp.arange(D, dtype=jnp.float32) / (D - 1)
    col_scale = jnp.exp(jax.random.uniform(key_cols, (D,), jnp.float32, -0.693, 0.693)) * ramp
    row_scale = jnp.exp(jax.random.uniform(key_rows, (EDGES, 1), jnp.float32, 0.0, 2.3))
    base_draw = jax.random.truncated_normal(key_base, -4.0, 4.0, (EDGES, D), jnp.float32)
    row_shift = 0.5 * jax.random.truncated_normal(key_shift, -4.0, 4.0, (EDGES, 1), jnp.float32)
    result = (base_draw * col_scale + row_shift) * row_scale
    return result.astype(jnp.bfloat16)


def block_levels(own_key, extent, pieces, low, largest):
    level, own = 1.0, jax.random.fold_in(own_key, 6)
    for position, parts in pieces:
        heights = jnp.exp(jax.random.uniform(jax.random.fold_in(own, position), (parts,), jnp.float32, low / len(pieces), largest / len(pieces)))
        level = level * jnp.repeat(heights, extent[position] // parts).reshape([-1 if axis == position else 1 for axis in range(len(extent))])
    return level


def scatter_about(key, dims, width, reach, cuts=(), held_as=jnp.bfloat16):
    entries = jax.random.normal(key, dims, jnp.float32) * width
    if len(cuts) > 0:
        entries = block_levels(key, dims, cuts, -0.22, 0.18) * entries
    return jnp.clip(entries, min=-reach, max=reach).astype(held_as)


def setup_inputs(seed: int = 0, part: int = 0) -> dict:
    streams_of = jax.random.split(jax.random.key(seed), 13)
    own_keys = jax.random.split(jax.random.fold_in(streams_of[12], part), 13)
    node_latents = scatter_about(own_keys[0], (NODES, D), 1.0, 6.0, ((0, 4), (1, 2)))
    edge_latents = scatter_about(own_keys[1], (EDGES, D), 1.0, 6.0, ((0, 4), (1, 2)))
    sender_latents = scatter_about(own_keys[2], (EDGES, D), 1.0, 6.0, ((0, 4), (1, 2)))
    pre_hidden = scatter_about(own_keys[3], (EDGES, H), 1.5, 6.0, ((0, 4), (1, 2)))
    pre_norm = draw_pre_norm(jax.random.fold_in(jax.random.fold_in(streams_of[12], part), 71), part)
    norm_gain = jnp.clip(0.5 + 1.0 * jax.random.uniform(streams_of[5], (D,), jnp.float32) ** block_levels(streams_of[5], (D,), ((0, 2),), -0.2, 0.2), 0.5, 1.5)
    w_in = scatter_about(streams_of[6], (3, D, H), (3 * D) ** -0.5, 0.15625, ((1, 2),))
    w_out = scatter_about(streams_of[7], (H, D), H ** -0.5, 0.25, ((0, 2), (1, 2)))
    senders = draw_senders(jax.random.fold_in(jax.random.fold_in(streams_of[12], part), 71), part)
    receivers = draw_receivers(jax.random.fold_in(jax.random.fold_in(streams_of[12], part), 71), part)
    edge_cotangent = scatter_about(own_keys[10], (EDGES, D), 1.0, 6.0, ((0, 4), (1, 2)))
    agg_cotangent = scatter_about(own_keys[11], (NODES, D), 1.0, 6.0, ((0, 4), (1, 2)))
    return dict(node_latents=node_latents, edge_latents=edge_latents, sender_latents=sender_latents, pre_hidden=pre_hidden, pre_norm=pre_norm, norm_gain=norm_gain, w_in=w_in, w_out=w_out, senders=senders, receivers=receivers, edge_cotangent=edge_cotangent, agg_cotangent=agg_cotangent)


def silu_parts(pre_hidden):
    pre_value = pre_hidden.astype(jnp.float32)
    sig_value = jax.nn.sigmoid(pre_value)
    activation = (pre_value * sig_value).astype(jnp.bfloat16)
    derivative = sig_value * (1.0 + pre_value * (1.0 - sig_value))
    return (activation, derivative)

def reference(node_latents, edge_latents, sender_latents, pre_hidden, pre_norm, norm_gain, w_in, w_out, senders, receivers, edge_cotangent, agg_cotangent):
    grad_scale = 1.0 / math.sqrt(EDGES)
    activation, derivative = silu_parts(pre_hidden)
    stored = pre_norm.astype(jnp.float32)
    row_mean = lax.optimization_barrier(jnp.mean(stored, axis=1, keepdims=True))
    centered = stored - row_mean
    row_var = lax.optimization_barrier(jnp.mean(centered * centered, axis=1, keepdims=True))
    inv_std = lax.rsqrt(row_var + 1e-05)
    normed = centered * inv_std
    upstream = edge_cotangent.astype(jnp.float32) + agg_cotangent.astype(jnp.float32)[receivers]
    weighted = norm_gain * upstream
    mean_first = lax.optimization_barrier(jnp.mean(weighted, axis=1, keepdims=True))
    mean_cross = lax.optimization_barrier(jnp.mean(weighted * normed, axis=1, keepdims=True))
    norm_grad = (inv_std * (weighted - mean_first - normed * mean_cross)).astype(jnp.bfloat16)
    hidden_grad = jnp.dot(norm_grad, w_out.T, preferred_element_type=jnp.float32)
    pre_grad = (hidden_grad * derivative).astype(jnp.bfloat16)
    w_flat = w_in.reshape(3 * D, H)
    input_grad = jnp.dot(pre_grad, w_flat.T, preferred_element_type=jnp.float32).reshape(EDGES, 3, D)
    edge_grad = (edge_cotangent.astype(jnp.float32) + input_grad[:, 0, :]).astype(jnp.bfloat16)
    sender_term = lax.optimization_barrier(input_grad[:, 1, :].astype(jnp.bfloat16)).astype(jnp.float32)
    node_grad = jax.ops.segment_sum(input_grad[:, 2, :], receivers, num_segments=NODES)
    node_grad = node_grad + jax.ops.segment_sum(sender_term, senders, num_segments=NODES)
    inputs = jnp.concatenate([edge_latents, sender_latents, node_latents[receivers]], axis=1)
    w_in_grad = (jnp.dot(inputs.T, pre_grad, preferred_element_type=jnp.float32) * grad_scale).reshape(3, D, H)
    w_out_grad = jnp.dot(activation.T, norm_grad, preferred_element_type=jnp.float32) * grad_scale
    gain_grad = lax.optimization_barrier(jnp.sum(upstream * normed, axis=0)) * grad_scale
    return (node_grad, edge_grad, w_in_grad, w_out_grad, gain_grad)
```

```python
import functools
import math

import jax
import jax.numpy as jnp
from jax import lax
from jax.experimental import pallas as pl
from jax.experimental.pallas import tpu as pltpu
from jax.sharding import PartitionSpec as P

F32 = jnp.float32
BF16 = jnp.bfloat16
VMEM_LIMIT = 48 * 1024 * 1024
PAD = 16


def dot_nn(a, b):
    return lax.dot_general(a, b, (((1,), (0,)), ((), ())), preferred_element_type=F32)


def dot_nt(a, b):
    return lax.dot_general(a, b, (((1,), (1,)), ((), ())), preferred_element_type=F32)


def dot_tn(a, b):
    return lax.dot_general(a, b, (((0,), (0,)), ((), ())), preferred_element_type=F32)


def params():
    return pltpu.CompilerParams(vmem_limit_bytes=VMEM_LIMIT)


def cost(flops, nbytes):
    return pl.CostEstimate(flops=int(flops), bytes_accessed=int(nbytes), transcendentals=0)


def whole(shape):
    return pl.BlockSpec(shape, lambda *_: (0,) * len(shape))


def ring(size, step):
    return [(i, (i + step) % size) for i in range(size)]


def split_rows(row, width):
    parts = [row[:, j * width : (j + 1) * width] for j in range(row.shape[1] // width)]
    parts.append(jnp.zeros((PAD - len(parts), width), row.dtype))
    return jnp.concatenate(parts, axis=0)


def edge_kernel(
    nodes_dev, steps, idx, x_own, x_sib, cot_own, cot_sib, hid, recv, agg_own, agg_sib, gain_own, gain_sib,
    w_own, w_sib, pre_grad, wo_own, gain_out, small, acc_sib, gsum_own, gsum_sib,
):
    step = pl.program_id(0)
    first_node = idx[1] * nodes_dev
    rows, half_width = x_own.shape
    width = 2 * half_width

    @pl.when(step == 0)
    def _():
        wo_own[...] = jnp.zeros_like(wo_own)
        acc_sib[...] = jnp.zeros_like(acc_sib)
        gsum_own[...] = jnp.zeros_like(gsum_own)
        gsum_sib[...] = jnp.zeros_like(gsum_sib)

    column = jnp.transpose(jnp.broadcast_to(recv[...], (8, rows)))[:, :1] - first_node
    picks = lax.broadcasted_iota(jnp.int32, (rows, nodes_dev), 1) == column
    picks = jnp.where(picks, 1.0, 0.0).astype(BF16)
    up_own = cot_own[...].astype(F32) + dot_nn(picks, agg_own[...])
    up_sib = cot_sib[...].astype(F32) + dot_nn(picks, agg_sib[...])

    def row_mean(a, b):
        return jnp.sum(a + b, axis=1, keepdims=True) * (1.0 / width)

    v_own = x_own[...].astype(F32)
    v_sib = x_sib[...].astype(F32)
    mean = row_mean(v_own, v_sib)
    v_own = v_own - mean
    v_sib = v_sib - mean
    inv = lax.rsqrt(row_mean(v_own * v_own, v_sib * v_sib) + 1e-05)
    n_own = v_own * inv
    n_sib = v_sib * inv
    wt_own = gain_own[...] * up_own
    wt_sib = gain_sib[...] * up_sib
    mean_first = row_mean(wt_own, wt_sib)
    mean_cross = row_mean(wt_own * n_own, wt_sib * n_sib)
    g_own = (inv * (wt_own - mean_first - n_own * mean_cross)).astype(BF16)
    g_sib = (inv * (wt_sib - mean_first - n_sib * mean_cross)).astype(BF16)
    hidden = dot_nt(g_own, w_own[...]) + dot_nt(g_sib, w_sib[...])
    value = hid[...].astype(F32)
    sig = 1.0 / (1.0 + jnp.exp(-value))
    act = (value * sig).astype(BF16)
    pre_grad[...] = (hidden * (sig * (1.0 + value * (1.0 - sig)))).astype(BF16)
    wo_own[...] += dot_tn(g_own, act)
    acc_sib[...] += dot_tn(g_sib, act)
    gsum_own[...] += jnp.sum(up_own * n_own, axis=0, keepdims=True)
    gsum_sib[...] += jnp.sum(up_sib * n_sib, axis=0, keepdims=True)

    @pl.when(step == steps - 1)
    def _():
        gain_out[...] = gsum_own[...]
        small[: acc_sib.shape[0], :] = acc_sib[...].astype(BF16)
        small[acc_sib.shape[0] :, :] = split_rows(gsum_sib[...], small.shape[1]).astype(BF16)


def pool_kernel(
    shards, steps, idx, g_own, g_sib, edge_lat, send_lat, node_lat, senders, recv, wo_own, gain_own, small, *rest
):
    w_out = rest[:shards]
    s_out = rest[shards : 2 * shards]
    recv_out, grads, pooled, by_recv = rest[2 * shards :]
    step = pl.program_id(0)
    core, shard = idx[0], idx[1]
    nodes_dev, half_width = node_lat.shape
    half_nodes = nodes_dev // 2
    rows, feat_width = g_own.shape

    @pl.when(step == 0)
    def _():
        grads[...] = jnp.zeros_like(grads)
        pooled[...] = jnp.zeros_like(pooled)
        by_recv[...] = jnp.zeros_like(by_recv)

    grad = jnp.where(step < steps // 2, g_own[...], g_sib[...])
    node_id = lax.broadcasted_iota(jnp.int32, (nodes_dev, rows), 0)
    picks = jnp.where(node_id + shard * nodes_dev == recv[...], 1.0, 0.0).astype(BF16)
    by_recv[...] += dot_nn(picks, grad)
    half_id = lax.broadcasted_iota(jnp.int32, (half_nodes, rows), 0) + core * half_nodes
    for dest in range(shards):
        picks = jnp.where(half_id + dest * nodes_dev == senders[...], 1.0, 0.0).astype(BF16)
        pooled[dest * half_nodes : (dest + 1) * half_nodes, :] += dot_nn(picks, grad)
    grads[:half_width, :] += dot_tn(edge_lat[...], grad)
    grads[half_width : 2 * half_width, :] += dot_tn(send_lat[...], grad)

    @pl.when(step == steps - 1)
    def _():
        sums = by_recv[...]
        high = sums.astype(BF16)
        low = (sums - high.astype(F32)).astype(BF16)
        grads[2 * half_width : 3 * half_width, :] = dot_tn(node_lat[...], high) + dot_tn(node_lat[...], low)
        grads[3 * half_width :, :] = wo_own[...] + small[:half_width, :].astype(F32)
        gain = split_rows(gain_own[...], feat_width) + small[half_width:, :].astype(F32)
        recv_out[...] = high
        block = 4 * half_width // shards
        for k in range(shards):
            dest = lax.rem(shard + k, shards)
            w_rows = grads[pl.ds(pl.multiple_of(dest * block, 16), block), :]
            w_out[k][:block, :] = w_rows.astype(w_out[k].dtype)
            w_out[k][block:, :] = gain.astype(w_out[k].dtype)
            s_rows = pooled[pl.ds(pl.multiple_of(dest * half_nodes, 16), half_nodes), :]
            s_out[k][...] = s_rows.astype(s_out[k].dtype)


def sum_kernel(*refs):
    total = refs[0][...].astype(F32)
    for ref in refs[1:-1]:
        total = total + ref[...].astype(F32)
    refs[-1][...] = total.astype(refs[-1].dtype)


def add_up(parts):
    return pl.pallas_call(
        sum_kernel,
        out_shape=jax.ShapeDtypeStruct(parts[0].shape, BF16),
        compiler_params=params(),
        cost_estimate=cost(parts[0].size * len(parts), parts[0].size * 10),
    )(*parts)


def sum_send_kernel(idx, by_recv, *refs):
    total = refs[0][...].astype(F32)
    for ref in refs[1:-2]:
        total = total + ref[...].astype(F32)
    alone, both = refs[-2:]
    total = total.astype(BF16)
    rows = total.shape[0]
    alone[...] = total
    both[:rows, :] = total
    both[rows:, :] = by_recv[pl.ds(pl.multiple_of(idx[0] * rows, 16), rows), :]


def place_kernel(shards, scale, idx, *refs):
    totals = refs[:shards]
    w_in_grad, w_out_grad, gain_grad, held = refs[shards:]
    half_width, feat_width = w_in_grad.shape[1:]
    block = 4 * half_width // shards
    for k in range(shards):
        source = lax.rem(idx[1] - k + shards, shards)
        held[pl.ds(pl.multiple_of(source * block, 16), block), :] = totals[k][:block, :].astype(F32) * scale

        @pl.when(source == 0)
        def _(k=k):
            rows = totals[k][block:, :].astype(F32) * scale
            for j in range(half_width // feat_width):
                gain_grad[:, j * feat_width : (j + 1) * feat_width] = rows[j : j + 1, :]

    for k in range(3):
        w_in_grad[k] = held[k * half_width : (k + 1) * half_width, :]
    w_out_grad[...] = jnp.transpose(held[3 * half_width :, :])


def edge_out_kernel(feats, steps, idx, cot, w_edge, *refs):
    own = refs[:feats]
    sib = refs[feats : 2 * feats]
    out, held = refs[2 * feats :]
    step = pl.program_id(0)
    feat_width = own[0].shape[1]
    for k in range(feats):
        source = lax.rem(idx[2] - k + feats, feats)
        piece = jnp.where(step < steps // 2, own[k][...], sib[k][...])
        held[:, pl.ds(pl.multiple_of(source * feat_width, 128), feat_width)] = piece
    out[...] = (cot[...].astype(F32) + dot_nt(held[...], w_edge[...])).astype(BF16)


def node_out_kernel(feats, idx, by_recv, w_send, w_recv, *refs):
    sums = refs[:2]
    crossed = refs[2 : 2 + 2 * (feats - 1)]
    out, held_send, held_recv = refs[-3:]
    rows, feat_width = sums[0].shape
    core, feat = idx[0], idx[2]
    mine = pl.ds(pl.multiple_of(feat * feat_width, 128), feat_width)
    held_recv[:, mine] = by_recv[...]
    for side in range(2):
        at = pl.ds(pl.multiple_of((core if side == 0 else 1 - core) * rows, 16), rows)
        held_send[at, mine] = sums[side][...]
        for k in range(1, feats):
            source = lax.rem(feat - k + feats, feats)
            there = pl.ds(pl.multiple_of(source * feat_width, 128), feat_width)
            held_send[at, there] = crossed[2 * (k - 1) + side][:rows, :]
            held_recv[at, there] = crossed[2 * (k - 1) + side][rows:, :]
    out[...] = dot_nt(held_send[...], w_send[...]) + dot_nt(held_recv[...], w_recv[...])


def body(
    node_latents, edge_latents, sender_latents, pre_hidden, pre_norm, norm_gain, w_in, w_out, senders, receivers,
    edge_cotangent, agg_cotangent,
):
    shards = lax.axis_size("nodes")
    feats = lax.axis_size("feat")
    core, shard, feat = (lax.axis_index(name) for name in ("chan", "nodes", "feat"))
    idx = jnp.stack([core, shard, feat]).astype(jnp.int32)
    nodes_dev, half_width = node_latents.shape
    edges = edge_latents.shape[0]
    feat_width = pre_hidden.shape[1]
    hidden_width = w_in.shape[2]
    half = edges // 2
    half_nodes = nodes_dev // 2
    scale = 1.0 / math.sqrt(edges * shards)

    def over_chan(x):
        return lax.ppermute(x, "chan", [(0, 1), (1, 0)])

    theirs = (1 - core) * half
    gap = -(2 * half + nodes_dev) % feat_width
    sent = jnp.concatenate(
        [
            lax.dynamic_slice_in_dim(pre_norm, theirs, half),
            lax.dynamic_slice_in_dim(edge_cotangent, theirs, half),
            agg_cotangent,
            jnp.zeros((gap, half_width), BF16),
            w_out,
        ]
    )
    got = over_chan(sent)
    gain_own = norm_gain.reshape(1, half_width)
    gain_sib = over_chan(gain_own)
    recv_row = receivers.reshape(1, edges)
    send_row = senders.reshape(1, edges)

    tile = 512
    steps = half // tile
    wide = (tile, half_width)
    narrow = (tile, feat_width)
    own = lambda i, s: (s[0] * steps + i, 0)
    pre_own, wo_own, gain_sum, small = pl.pallas_call(
        functools.partial(edge_kernel, nodes_dev, steps),
        grid_spec=pltpu.PrefetchScalarGridSpec(
            num_scalar_prefetch=1,
            grid=(steps,),
            in_specs=[
                pl.BlockSpec(wide, own),
                pl.BlockSpec(wide, lambda i, s: (i, 0)),
                pl.BlockSpec(wide, own),
                pl.BlockSpec(wide, lambda i, s: (steps + i, 0)),
                pl.BlockSpec(narrow, own),
                pl.BlockSpec((1, tile), lambda i, s: (0, s[0] * steps + i)),
                whole((nodes_dev, half_width)),
                pl.BlockSpec((nodes_dev, half_width), lambda i, s: (2 * half // nodes_dev, 0)),
                whole((1, half_width)),
                whole((1, half_width)),
                whole((feat_width, half_width)),
                pl.BlockSpec((feat_width, half_width), lambda i, s: ((2 * half + nodes_dev + gap) // feat_width, 0)),
            ],
            out_specs=[
                pl.BlockSpec(narrow, lambda i, s: (i, 0)),
                whole((half_width, feat_width)),
                whole((1, half_width)),
                whole((half_width + PAD, feat_width)),
            ],
            scratch_shapes=[
                pltpu.VMEM((half_width, feat_width), F32),
                pltpu.VMEM((1, half_width), F32),
                pltpu.VMEM((1, half_width), F32),
            ],
        ),
        out_shape=[
            jax.ShapeDtypeStruct((half, feat_width), BF16),
            jax.ShapeDtypeStruct((half_width, feat_width), F32),
            jax.ShapeDtypeStruct((1, half_width), F32),
            jax.ShapeDtypeStruct((half_width + PAD, feat_width), BF16),
        ],
        compiler_params=params(),
        cost_estimate=cost(4 * half * (nodes_dev + 2 * feat_width) * half_width, 10 * half * half_width),
        name="edge_norm",
    )(
        idx, pre_norm, got, edge_cotangent, got, pre_hidden, recv_row, agg_cotangent, got, gain_own, gain_sib,
        w_out, got,
    )

    pre_sib = over_chan(pre_own)
    small_sib = over_chan(small)
    crossed_own = [pre_own] + [lax.ppermute(pre_own, "feat", ring(feats, k)) for k in range(1, feats)]
    crossed_sib = [pre_sib] + [over_chan(x) for x in crossed_own[1:]]

    def by_edge(i, s):
        return jnp.where(i < steps, s[0] * steps + i, (1 - s[0]) * steps + i - steps)

    def first_half(i, s):
        return (jnp.minimum(i, steps - 1), 0)

    def second_half(i, s):
        return (jnp.maximum(i - steps, 0), 0)

    block = 4 * half_width // shards
    w_shapes = [
        jax.ShapeDtypeStruct((block + PAD, feat_width), F32 if k == 0 else BF16) for k in range(shards)
    ]
    s_shapes = [jax.ShapeDtypeStruct((half_nodes, feat_width), F32 if k == 0 else BF16) for k in range(shards)]
    pool_outs = w_shapes + s_shapes + [jax.ShapeDtypeStruct((nodes_dev, feat_width), BF16)]
    pooled = pl.pallas_call(
        functools.partial(pool_kernel, shards, 2 * steps),
        grid_spec=pltpu.PrefetchScalarGridSpec(
            num_scalar_prefetch=1,
            grid=(2 * steps,),
            in_specs=[
                pl.BlockSpec(narrow, first_half),
                pl.BlockSpec(narrow, second_half),
                pl.BlockSpec(wide, lambda i, s: (by_edge(i, s), 0)),
                pl.BlockSpec(wide, lambda i, s: (by_edge(i, s), 0)),
                whole((nodes_dev, half_width)),
                pl.BlockSpec((1, tile), lambda i, s: (0, by_edge(i, s))),
                pl.BlockSpec((1, tile), lambda i, s: (0, by_edge(i, s))),
                whole((half_width, feat_width)),
                whole((1, half_width)),
                whole((half_width + PAD, feat_width)),
            ],
            out_specs=[whole(x.shape) for x in pool_outs],
            scratch_shapes=[
                pltpu.VMEM((4 * half_width, feat_width), F32),
                pltpu.VMEM((shards * half_nodes, feat_width), F32),
                pltpu.VMEM((nodes_dev, feat_width), F32),
            ],
        ),
        out_shape=pool_outs,
        compiler_params=params(),
        cost_estimate=cost(
            2 * edges * feat_width * (nodes_dev + shards * half_nodes + 2 * half_width), 8 * edges * half_width
        ),
        name="pool",
    )(
        idx, pre_own, pre_sib, edge_latents, sender_latents, node_latents, send_row, recv_row, wo_own, gain_sum,
        small_sib,
    )
    w_parts, s_parts, by_recv = pooled[:shards], pooled[shards : 2 * shards], pooled[-1]

    w_got = [w_parts[0]] + [lax.ppermute(w_parts[k], "nodes", ring(shards, k)) for k in range(1, shards)]
    w_total = add_up(w_got)
    s_got = [s_parts[0]] + [lax.ppermute(s_parts[k], "nodes", ring(shards, k)) for k in range(1, shards)]
    w_all = [w_total] + [lax.ppermute(w_total, "nodes", ring(shards, k)) for k in range(1, shards)]
    smem = pl.BlockSpec(memory_space=pltpu.SMEM)
    vmem = pl.BlockSpec(memory_space=pltpu.VMEM)

    s_alone, s_both = pl.pallas_call(
        sum_send_kernel,
        in_specs=[smem] + [vmem] * (1 + shards),
        out_shape=[
            jax.ShapeDtypeStruct((half_nodes, feat_width), BF16),
            jax.ShapeDtypeStruct((nodes_dev, feat_width), BF16),
        ],
        compiler_params=params(),
        cost_estimate=cost(half_nodes * feat_width * shards, 10 * half_nodes * feat_width),
        name="sum_send",
    )(idx, by_recv, *s_got)
    s_cross = []
    for k in range(1, feats):
        from_feat = lax.ppermute(s_both, "feat", ring(feats, k))
        s_cross += [from_feat, over_chan(from_feat)]
    s_sib = over_chan(s_alone)

    edge_grad = pl.pallas_call(
        functools.partial(edge_out_kernel, feats, 2 * steps),
        grid_spec=pltpu.PrefetchScalarGridSpec(
            num_scalar_prefetch=1,
            grid=(2 * steps,),
            in_specs=[
                pl.BlockSpec(wide, lambda i, s: (by_edge(i, s), 0)),
                pl.BlockSpec((None, half_width, hidden_width), lambda i, s: (0, 0, 0)),
            ]
            + [pl.BlockSpec(narrow, first_half)] * feats
            + [pl.BlockSpec(narrow, second_half)] * feats,
            out_specs=pl.BlockSpec(wide, lambda i, s: (by_edge(i, s), 0)),
            scratch_shapes=[pltpu.VMEM((tile, hidden_width), BF16)],
        ),
        out_shape=jax.ShapeDtypeStruct((edges, half_width), BF16),
        compiler_params=params(),
        cost_estimate=cost(2 * edges * hidden_width * half_width, 8 * edges * half_width),
        name="edge_out",
    )(idx, edge_cotangent, w_in, *crossed_own, *crossed_sib)

    node_grad = pl.pallas_call(
        functools.partial(node_out_kernel, feats),
        grid=(1,),
        in_specs=[
            smem,
            whole((nodes_dev, feat_width)),
            pl.BlockSpec((None, half_width, hidden_width), lambda *_: (1, 0, 0)),
            pl.BlockSpec((None, half_width, hidden_width), lambda *_: (2, 0, 0)),
            whole((half_nodes, feat_width)),
            whole((half_nodes, feat_width)),
        ]
        + [whole((nodes_dev, feat_width))] * (2 * (feats - 1)),
        out_specs=whole((nodes_dev, half_width)),
        out_shape=jax.ShapeDtypeStruct((nodes_dev, half_width), F32),
        scratch_shapes=[
            pltpu.VMEM((nodes_dev, hidden_width), BF16),
            pltpu.VMEM((nodes_dev, hidden_width), BF16),
        ],
        compiler_params=params(),
        cost_estimate=cost(4 * nodes_dev * hidden_width * half_width, 8 * nodes_dev * hidden_width),
        name="node_out",
    )(idx, by_recv, w_in, w_in, s_alone, s_sib, *s_cross)

    w_in_grad, w_out_grad, gain_grad = pl.pallas_call(
        functools.partial(place_kernel, shards, scale),
        in_specs=[smem] + [vmem] * shards,
        out_shape=[
            jax.ShapeDtypeStruct((3, half_width, feat_width), F32),
            jax.ShapeDtypeStruct((feat_width, half_width), F32),
            jax.ShapeDtypeStruct((1, half_width), F32),
        ],
        scratch_shapes=[pltpu.VMEM((4 * half_width, feat_width), F32)],
        compiler_params=params(),
        cost_estimate=cost(8 * half_width * feat_width, 24 * half_width * feat_width),
        name="place",
    )(idx, *w_all)
    return (node_grad, edge_grad, w_in_grad, w_out_grad, gain_grad.reshape(half_width))


def solution(mesh):
    placed = (
        P(("groups", "nodes"), "chan"),
        P(("groups", "nodes"), "chan"),
        P(("groups", "nodes"), "chan"),
        P(("groups", "nodes"), "feat"),
        P(("groups", "nodes"), "chan"),
        P("chan"),
        P(None, "chan", None),
        P("feat", "chan"),
        P(("groups", "nodes")),
        P(("groups", "nodes")),
        P(("groups", "nodes"), "chan"),
        P(("groups", "nodes"), "chan"),
    )
    return jax.shard_map(
        body,
        mesh=mesh,
        in_specs=placed,
        out_specs=(
            P(("groups", "nodes"), "chan"),
            P(("groups", "nodes"), "chan"),
            P("groups", "chan", "feat"),
            P(("groups", "feat"), "chan"),
            P(("groups", "chan")),
        ),
        check_vma=False,
    )
```

```python
import functools
import math

import jax
import jax.numpy as jnp
from jax import lax
from jax.experimental import pallas as pl
from jax.experimental.pallas import tpu as pltpu
from jax.sharding import PartitionSpec as P

F32 = jnp.float32
BF16 = jnp.bfloat16
PAD = 16


def dot_nn(a, b):
    return lax.dot_general(a, b, (((1,), (0,)), ((), ())), preferred_element_type=F32)


def dot_nt(a, b):
    return lax.dot_general(a, b, (((1,), (1,)), ((), ())), preferred_element_type=F32)


def dot_tn(a, b):
    return lax.dot_general(a, b, (((0,), (0,)), ((), ())), preferred_element_type=F32)


def params(mib=48):
    return pltpu.CompilerParams(vmem_limit_bytes=mib * 1024 * 1024)


def cost(flops, nbytes):
    return pl.CostEstimate(flops=int(flops), bytes_accessed=int(nbytes), transcendentals=0)


def whole(shape):
    return pl.BlockSpec(shape, lambda *_: (0,) * len(shape))


def in_hbm(x):
    return pltpu.with_memory_space_constraint(x, pltpu.HBM)


def ring(size, step):
    return [(i, (i + step) % size) for i in range(size)]


def split_rows(row, width):
    parts = [row[:, j * width : (j + 1) * width] for j in range(row.shape[1] // width)]
    parts.append(jnp.zeros((PAD - len(parts), width), row.dtype))
    return jnp.concatenate(parts, axis=0)


def edge_kernel(steps, idx, *refs):
    small_in, tiled_in = refs[:7], refs[7:12]
    pre_grad, wo_own, gain_out, small = refs[12:16]
    small_held, tiled_held = refs[16:23], refs[23:28]
    acc_sib, small_sems, tiled_sems = refs[28:]
    half, feat_width = pre_grad.shape
    rows = half // steps
    first = pl.multiple_of(idx[0] * half, 128)

    def tile_copies(step):
        out = []
        for j, (src, dst) in enumerate(zip(tiled_in, tiled_held)):
            here = pl.ds(step * rows, rows)
            there = pl.ds(pl.multiple_of(first + step * rows, 128), rows)
            out.append(pltpu.make_async_copy(src.at[there, :], dst.at[here, :], tiled_sems.at[j, step]))
        return out

    small_copies = []
    for j, (src, dst) in enumerate(zip(small_in, small_held)):
        if j == 0:
            src = src.at[:, pl.ds(first, half)]
        small_copies.append(pltpu.make_async_copy(src, dst, small_sems.at[j]))
    tiles = [tile_copies(step) for step in range(steps)]
    for copy in small_copies[:3] + tiles[0] + small_copies[3:]:
        copy.start()
    for copies in tiles[1:]:
        for copy in copies:
            copy.start()
    for copy in small_copies:
        copy.wait()

    recv, agg_own, agg_sib, gain_own, gain_sib, w_own, w_sib = small_held
    nodes_dev, half_width = agg_own.shape
    width = 2 * half_width
    first_node = idx[1] * nodes_dev
    gsum_own = jnp.zeros((1, half_width), F32)
    gsum_sib = jnp.zeros((1, half_width), F32)

    def row_mean(a, b):
        return jnp.sum(a + b, axis=1, keepdims=True) * (1.0 / width)

    for step in range(steps):
        at = slice(step * rows, (step + 1) * rows)
        column = jnp.transpose(jnp.broadcast_to(recv[:, at], (8, rows)))[:, :1] - first_node
        picks = lax.broadcasted_iota(jnp.int32, (rows, nodes_dev), 1) == column
        picks = jnp.where(picks, 1.0, 0.0).astype(BF16)
        for copy in tiles[step]:
            copy.wait()
        x_own, x_sib, cot_own, cot_sib, hid = (ref[at, :] for ref in tiled_held)
        v_own = x_own.astype(F32)
        v_sib = x_sib.astype(F32)
        mean = row_mean(v_own, v_sib)
        v_own = v_own - mean
        v_sib = v_sib - mean
        inv = lax.rsqrt(row_mean(v_own * v_own, v_sib * v_sib) + 1e-05)
        n_own = v_own * inv
        n_sib = v_sib * inv
        up_own = cot_own.astype(F32) + dot_nn(picks, agg_own[...])
        up_sib = cot_sib.astype(F32) + dot_nn(picks, agg_sib[...])
        wt_own = gain_own[...] * up_own
        wt_sib = gain_sib[...] * up_sib
        mean_first = row_mean(wt_own, wt_sib)
        mean_cross = row_mean(wt_own * n_own, wt_sib * n_sib)
        g_own = (inv * (wt_own - mean_first - n_own * mean_cross)).astype(BF16)
        g_sib = (inv * (wt_sib - mean_first - n_sib * mean_cross)).astype(BF16)
        hidden = dot_nt(g_own, w_own[...]) + dot_nt(g_sib, w_sib[...])
        value = hid.astype(F32)
        sig = 1.0 / (1.0 + jnp.exp(-value))
        act = (value * sig).astype(BF16)
        pre_grad[at, :] = (hidden * (sig * (1.0 + value * (1.0 - sig)))).astype(BF16)
        if step == 0:
            wo_own[...] = dot_tn(g_own, act)
            acc_sib[...] = dot_tn(g_sib, act)
        else:
            wo_own[...] += dot_tn(g_own, act)
            acc_sib[...] += dot_tn(g_sib, act)
        gsum_own = gsum_own + jnp.sum(up_own * n_own, axis=0, keepdims=True)
        gsum_sib = gsum_sib + jnp.sum(up_sib * n_sib, axis=0, keepdims=True)

    gain_out[...] = gsum_own
    small[:half_width, :] = acc_sib[...].astype(BF16)
    small[half_width:, :] = split_rows(gsum_sib, feat_width).astype(BF16)


def pool_kernel(
    shards, steps, idx, g_own, g_sib, edge_lat, send_lat, node_lat, senders, recv, wo_own, gain_own, small, *rest
):
    outs = rest[:shards]
    recv_out, grads, pooled, by_recv = rest[shards:]
    step = pl.program_id(0)
    core, shard = idx[0], idx[1]
    nodes_dev, half_width = node_lat.shape
    half_nodes = nodes_dev // 2
    rows, feat_width = g_own.shape

    @pl.when(step == 0)
    def _():
        grads[...] = jnp.zeros_like(grads)
        pooled[...] = jnp.zeros_like(pooled)
        by_recv[...] = jnp.zeros_like(by_recv)

    grad = jnp.where(step < steps // 2, g_own[...], g_sib[...])
    node_id = lax.broadcasted_iota(jnp.int32, (nodes_dev, rows), 0)
    picks = jnp.where(node_id + shard * nodes_dev == recv[...], 1.0, 0.0).astype(BF16)
    by_recv[...] += dot_nn(picks, grad)
    half_id = lax.broadcasted_iota(jnp.int32, (half_nodes, rows), 0) + core * half_nodes
    for dest in range(shards):
        picks = jnp.where(half_id + dest * nodes_dev == senders[...], 1.0, 0.0).astype(BF16)
        pooled[dest * half_nodes : (dest + 1) * half_nodes, :] += dot_nn(picks, grad)
    grads[:half_width, :] += dot_tn(edge_lat[...], grad)
    grads[half_width : 2 * half_width, :] += dot_tn(send_lat[...], grad)

    @pl.when(step == steps - 1)
    def _():
        sums = by_recv[...]
        high = sums.astype(BF16)
        low = (sums - high.astype(F32)).astype(BF16)
        grads[2 * half_width : 3 * half_width, :] = dot_tn(node_lat[...], high) + dot_tn(node_lat[...], low)
        grads[3 * half_width :, :] = wo_own[...] + small[:half_width, :].astype(F32)
        gain = split_rows(gain_own[...], feat_width) + small[half_width:, :].astype(F32)
        recv_out[...] = high
        block = 4 * half_width // shards
        for k in range(shards):
            dest = lax.rem(shard + k, shards)
            kind = outs[k].dtype
            w_rows = grads[pl.ds(pl.multiple_of(dest * block, 16), block), :]
            outs[k][:block, :] = w_rows.astype(kind)
            outs[k][block : block + PAD, :] = gain.astype(kind)
            s_rows = pooled[pl.ds(pl.multiple_of(dest * half_nodes, 16), half_nodes), :]
            outs[k][block + PAD :, :] = s_rows.astype(kind)


def sum_kernel(shards, *refs):
    w_total, s_total = refs[-2:]
    total = refs[0][...].astype(F32)
    for ref in refs[1:shards]:
        total = total + ref[...].astype(F32)
    rows = w_total.shape[0]
    w_total[...] = total[:rows].astype(BF16)
    s_total[...] = total[rows:].astype(BF16)


def place_kernel(shards, scale, idx, *refs):
    totals = refs[:shards]
    w_in_grad, w_out_grad, gain_grad, held = refs[-4:]
    half_width, feat_width = w_in_grad.shape[1:]
    block = 4 * half_width // shards
    for k in range(shards):
        source = lax.rem(idx[1] - k + shards, shards)
        held[pl.ds(pl.multiple_of(source * block, 16), block), :] = totals[k][:block, :].astype(F32) * scale

        @pl.when(source == 0)
        def _(k=k):
            rows = totals[k][block:, :].astype(F32) * scale
            for j in range(half_width // feat_width):
                gain_grad[:, j * feat_width : (j + 1) * feat_width] = rows[j : j + 1, :]

    for k in range(3):
        w_in_grad[k] = held[k * half_width : (k + 1) * half_width, :]
    w_out_grad[...] = jnp.transpose(held[3 * half_width :, :])


def edge_out_kernel(feats, steps, idx, cot, w_edge, *refs):
    own = refs[:feats]
    sib = refs[feats : 2 * feats]
    out, token, held = refs[2 * feats :]
    token[...] = jnp.zeros_like(token)
    step = pl.program_id(0)
    feat_width = own[0].shape[1]
    for k in range(feats):
        source = lax.rem(idx[2] - k + feats, feats)
        piece = jnp.where(step < steps // 2, own[k][...], sib[k][...])
        held[:, pl.ds(pl.multiple_of(source * feat_width, 128), feat_width)] = piece
    out[...] = (cot[...].astype(F32) + dot_nt(held[...], w_edge[...])).astype(BF16)


def node_out_kernel(feats, idx, w_send, w_recv, *refs):
    by_recv = refs[:feats]
    sums = refs[feats : 3 * feats]
    out, held_send, held_recv = refs[-3:]
    rows, feat_width = sums[0].shape
    for k in range(feats):
        source = lax.rem(idx[2] - k + feats, feats)
        there = pl.ds(pl.multiple_of(source * feat_width, 128), feat_width)
        held_recv[:, there] = by_recv[k][...]
        for side in range(2):
            at = pl.ds(pl.multiple_of((idx[0] if side == 0 else 1 - idx[0]) * rows, 16), rows)
            held_send[at, there] = sums[2 * k + side][...]
    out[...] = dot_nt(held_send[...], w_send[...]) + dot_nt(held_recv[...], w_recv[...])


def body(
    node_latents, edge_latents, sender_latents, pre_hidden, pre_norm, norm_gain, w_in, w_out, senders, receivers,
    edge_cotangent, agg_cotangent,
):
    shards = lax.axis_size("nodes")
    feats = lax.axis_size("feat")
    core, shard, feat = (lax.axis_index(name) for name in ("chan", "nodes", "feat"))
    idx = jnp.stack([core, shard, feat]).astype(jnp.int32)
    nodes_dev, half_width = node_latents.shape
    edges = edge_latents.shape[0]
    feat_width = pre_hidden.shape[1]
    hidden_width = w_in.shape[2]
    half = edges // 2
    half_nodes = nodes_dev // 2
    scale = 1.0 / math.sqrt(edges * shards)

    def over_chan(x):
        return lax.ppermute(x, "chan", [(0, 1), (1, 0)])

    pre_norm_sib = over_chan(pre_norm)
    cot_sib = over_chan(edge_cotangent)
    agg_sib = over_chan(agg_cotangent)
    w_out_sib = over_chan(w_out)
    gain_own = norm_gain.reshape(1, half_width)
    gain_sib = over_chan(gain_own)
    recv_row = receivers.reshape(1, edges)
    send_row = senders.reshape(1, edges)

    tile = 768
    steps = half // tile
    wide = (tile, half_width)
    narrow = (tile, feat_width)
    smem = pl.BlockSpec(memory_space=pltpu.SMEM)
    vmem = pl.BlockSpec(memory_space=pltpu.VMEM)
    edge_steps = 3
    pre_own, wo_own, gain_sum, small = pl.pallas_call(
        functools.partial(edge_kernel, edge_steps),
        in_specs=[smem] + [pl.BlockSpec(memory_space=pl.ANY)] * 12,
        out_specs=[vmem] * 4,
        out_shape=[
            jax.ShapeDtypeStruct((half, feat_width), BF16),
            jax.ShapeDtypeStruct((half_width, feat_width), F32),
            jax.ShapeDtypeStruct((1, half_width), F32),
            jax.ShapeDtypeStruct((half_width + PAD, feat_width), BF16),
        ],
        scratch_shapes=[
            pltpu.VMEM((1, half), jnp.int32),
            pltpu.VMEM((nodes_dev, half_width), BF16),
            pltpu.VMEM((nodes_dev, half_width), BF16),
            pltpu.VMEM((1, half_width), F32),
            pltpu.VMEM((1, half_width), F32),
            pltpu.VMEM((feat_width, half_width), BF16),
            pltpu.VMEM((feat_width, half_width), BF16),
            pltpu.VMEM((half, half_width), BF16),
            pltpu.VMEM((half, half_width), BF16),
            pltpu.VMEM((half, half_width), BF16),
            pltpu.VMEM((half, half_width), BF16),
            pltpu.VMEM((half, feat_width), BF16),
            pltpu.VMEM((half_width, feat_width), F32),
            pltpu.SemaphoreType.DMA((7,)),
            pltpu.SemaphoreType.DMA((5, edge_steps)),
        ],
        compiler_params=params(),
        cost_estimate=cost(4 * half * (nodes_dev + 2 * feat_width) * half_width, 10 * half * half_width),
        name="edge_norm",
    )(
        idx, in_hbm(recv_row), in_hbm(agg_cotangent), agg_sib, in_hbm(gain_own), gain_sib, in_hbm(w_out), w_out_sib,
        in_hbm(pre_norm), in_hbm(pre_norm_sib), in_hbm(edge_cotangent), in_hbm(cot_sib), in_hbm(pre_hidden),
    )

    pre_sib = over_chan(pre_own)
    small_sib = over_chan(small)
    crossed_own = [pre_own] + [lax.ppermute(pre_own, "feat", ring(feats, k)) for k in range(1, feats)]

    def by_edge(i, s):
        return jnp.where(i < steps, s[0] * steps + i, (1 - s[0]) * steps + i - steps)

    def first_half(i, s):
        return (jnp.minimum(i, steps - 1), 0)

    def second_half(i, s):
        return (jnp.maximum(i - steps, 0), 0)

    block = 4 * half_width // shards
    rows_out = block + PAD + half_nodes
    pool_outs = [jax.ShapeDtypeStruct((rows_out, feat_width), F32 if k == 0 else BF16) for k in range(shards)]
    pool_outs.append(jax.ShapeDtypeStruct((nodes_dev, feat_width), BF16))
    *parts, by_recv = pl.pallas_call(
        functools.partial(pool_kernel, shards, 2 * steps),
        grid_spec=pltpu.PrefetchScalarGridSpec(
            num_scalar_prefetch=1,
            grid=(2 * steps,),
            in_specs=[
                pl.BlockSpec(narrow, first_half),
                pl.BlockSpec(narrow, second_half),
                pl.BlockSpec(wide, lambda i, s: (by_edge(i, s), 0)),
                pl.BlockSpec(wide, lambda i, s: (by_edge(i, s), 0)),
                whole((nodes_dev, half_width)),
                pl.BlockSpec((1, tile), lambda i, s: (0, by_edge(i, s))),
                pl.BlockSpec((1, tile), lambda i, s: (0, by_edge(i, s))),
                whole((half_width, feat_width)),
                whole((1, half_width)),
                whole((half_width + PAD, feat_width)),
            ],
            out_specs=[whole(x.shape) for x in pool_outs],
            scratch_shapes=[
                pltpu.VMEM((4 * half_width, feat_width), F32),
                pltpu.VMEM((shards * half_nodes, feat_width), F32),
                pltpu.VMEM((nodes_dev, feat_width), F32),
            ],
        ),
        out_shape=pool_outs,
        compiler_params=params(),
        cost_estimate=cost(
            2 * edges * feat_width * (nodes_dev + shards * half_nodes + 2 * half_width), 8 * edges * half_width
        ),
        name="pool",
    )(
        idx, pre_own, pre_sib, edge_latents, sender_latents, node_latents, send_row, recv_row, wo_own, gain_sum,
        small_sib,
    )
    arrived = [parts[0]] + [lax.ppermute(parts[k], "nodes", ring(shards, k)) for k in range(1, shards)]
    recv_all = [by_recv] + [lax.ppermute(by_recv, "feat", ring(feats, k)) for k in range(1, feats)]
    w_total, s_total = pl.pallas_call(
        functools.partial(sum_kernel, shards),
        in_specs=[vmem] * shards + [pl.BlockSpec(memory_space=pl.ANY)] * (feats - 1),
        out_shape=[
            jax.ShapeDtypeStruct((block + PAD, feat_width), BF16),
            jax.ShapeDtypeStruct((half_nodes, feat_width), BF16),
        ],
        compiler_params=params(),
        cost_estimate=cost(rows_out * feat_width * shards, 4 * rows_out * feat_width * shards),
        name="sum_parts",
    )(*arrived, *recv_all[1:])
    w_all = [w_total] + [lax.ppermute(w_total, "nodes", ring(shards, k)) for k in range(1, shards)]
    s_all = [s_total, over_chan(s_total)]
    for k in range(1, feats):
        s_all.append(lax.ppermute(s_total, "feat", ring(feats, k)))
        flip = [(2 * f + c, 2 * ((f + k) % feats) + 1 - c) for f in range(feats) for c in range(2)]
        s_all.append(lax.ppermute(s_total, ("feat", "chan"), flip))

    passed, _ = lax.optimization_barrier((crossed_own[1:], s_total))
    crossed_own = [pre_own] + passed
    crossed_sib = [pre_sib] + [over_chan(x) for x in passed]

    edge_grad, edge_token = pl.pallas_call(
        functools.partial(edge_out_kernel, feats, 2 * steps),
        grid_spec=pltpu.PrefetchScalarGridSpec(
            num_scalar_prefetch=1,
            grid=(2 * steps,),
            in_specs=[
                pl.BlockSpec(wide, lambda i, s: (by_edge(i, s), 0)),
                pl.BlockSpec((None, half_width, hidden_width), lambda i, s: (0, 0, 0)),
            ]
            + [pl.BlockSpec(narrow, first_half)] * feats
            + [pl.BlockSpec(narrow, second_half)] * feats,
            out_specs=[pl.BlockSpec(wide, lambda i, s: (by_edge(i, s), 0)), whole((8, 128))],
            scratch_shapes=[pltpu.VMEM((tile, hidden_width), BF16)],
        ),
        out_shape=[jax.ShapeDtypeStruct((edges, half_width), BF16), jax.ShapeDtypeStruct((8, 128), F32)],
        compiler_params=params(),
        cost_estimate=cost(2 * edges * hidden_width * half_width, 8 * edges * half_width),
        name="edge_out",
    )(idx, edge_cotangent, w_in, *crossed_own, *crossed_sib)

    w_in_grad, w_out_grad, gain_grad = pl.pallas_call(
        functools.partial(place_kernel, shards, scale),
        in_specs=[smem] + [vmem] * shards + [pl.BlockSpec(memory_space=pl.ANY)],
        out_shape=[
            jax.ShapeDtypeStruct((3, half_width, feat_width), F32),
            jax.ShapeDtypeStruct((feat_width, half_width), F32),
            jax.ShapeDtypeStruct((1, half_width), F32),
        ],
        scratch_shapes=[pltpu.VMEM((4 * half_width, feat_width), F32)],
        compiler_params=params(),
        cost_estimate=cost(8 * half_width * feat_width, 24 * half_width * feat_width),
        name="place",
    )(idx, *w_all, edge_token)
    node_grad = pl.pallas_call(
        functools.partial(node_out_kernel, feats),
        grid=(1,),
        in_specs=[
            smem,
            pl.BlockSpec((None, half_width, hidden_width), lambda *_: (1, 0, 0)),
            pl.BlockSpec((None, half_width, hidden_width), lambda *_: (2, 0, 0)),
        ]
        + [whole((nodes_dev, feat_width))] * feats
        + [whole((half_nodes, feat_width))] * (2 * feats)
        + [pl.BlockSpec(memory_space=pl.ANY)],
        out_specs=whole((nodes_dev, half_width)),
        out_shape=jax.ShapeDtypeStruct((nodes_dev, half_width), F32),
        scratch_shapes=[
            pltpu.VMEM((nodes_dev, hidden_width), BF16),
            pltpu.VMEM((nodes_dev, hidden_width), BF16),
        ],
        compiler_params=params(),
        cost_estimate=cost(4 * nodes_dev * hidden_width * half_width, 8 * nodes_dev * hidden_width),
        name="node_out",
    )(idx, w_in, w_in, *recv_all, *s_all, gain_grad)

    return (node_grad, edge_grad, w_in_grad, w_out_grad, gain_grad.reshape(half_width))


def solution(mesh):
    placed = (
        P(("groups", "nodes"), "chan"),
        P(("groups", "nodes"), "chan"),
        P(("groups", "nodes"), "chan"),
        P(("groups", "nodes"), "feat"),
        P(("groups", "nodes"), "chan"),
        P("chan"),
        P(None, "chan", None),
        P("feat", "chan"),
        P(("groups", "nodes")),
        P(("groups", "nodes")),
        P(("groups", "nodes"), "chan"),
        P(("groups", "nodes"), "chan"),
    )
    return jax.shard_map(
        body,
        mesh=mesh,
        in_specs=placed,
        out_specs=(
            P(("groups", "nodes"), "chan"),
            P(("groups", "nodes"), "chan"),
            P("groups", "chan", "feat"),
            P(("groups", "feat"), "chan"),
            P(("groups", "chan")),
        ),
        check_vma=False,
    )
```

```python
import functools
import math

import jax
import jax.numpy as jnp
from jax import lax
from jax.experimental import pallas as pl
from jax.experimental.pallas import tpu as pltpu
from jax.sharding import PartitionSpec as P

F32 = jnp.float32
BF16 = jnp.bfloat16
PAD = 16


def dot_nn(a, b):
    return lax.dot_general(a, b, (((1,), (0,)), ((), ())), preferred_element_type=F32)


def dot_nt(a, b):
    return lax.dot_general(a, b, (((1,), (1,)), ((), ())), preferred_element_type=F32)


def dot_tn(a, b):
    return lax.dot_general(a, b, (((0,), (0,)), ((), ())), preferred_element_type=F32)


def params(mib=48):
    return pltpu.CompilerParams(vmem_limit_bytes=mib * 1024 * 1024)


def cost(flops, nbytes):
    return pl.CostEstimate(flops=int(flops), bytes_accessed=int(nbytes), transcendentals=0)


def whole(shape):
    return pl.BlockSpec(shape, lambda *_: (0,) * len(shape))


def in_hbm(x):
    return pltpu.with_memory_space_constraint(x, pltpu.HBM)


def ring(size, step):
    return [(i, (i + step) % size) for i in range(size)]


def split_rows(row, width):
    parts = [row[:, j * width : (j + 1) * width] for j in range(row.shape[1] // width)]
    parts.append(jnp.zeros((PAD - len(parts), width), row.dtype))
    return jnp.concatenate(parts, axis=0)


def edge_kernel(steps, idx, *refs):
    small_in, tiled_in = refs[:7], refs[7:12]
    pre_grad, wo_own, gain_out, small = refs[12:16]
    small_held, tiled_held = refs[16:23], refs[23:28]
    acc_sib, small_sems, tiled_sems = refs[28:]
    half, feat_width = pre_grad.shape
    rows = half // steps
    first = pl.multiple_of(idx[0] * half, 128)

    def tile_copies(step):
        out = []
        for j, (src, dst) in enumerate(zip(tiled_in, tiled_held)):
            here = pl.ds(step * rows, rows)
            there = pl.ds(pl.multiple_of(first + step * rows, 128), rows)
            out.append(pltpu.make_async_copy(src.at[there, :], dst.at[here, :], tiled_sems.at[j, step]))
        return out

    small_copies = []
    for j, (src, dst) in enumerate(zip(small_in, small_held)):
        if j == 0:
            src = src.at[:, pl.ds(first, half)]
        small_copies.append(pltpu.make_async_copy(src, dst, small_sems.at[j]))
    tiles = [tile_copies(step) for step in range(steps)]
    for copy in small_copies[:3] + tiles[0] + small_copies[3:]:
        copy.start()
    for copies in tiles[1:]:
        for copy in copies:
            copy.start()
    for copy in small_copies:
        copy.wait()

    recv, agg_own, agg_sib, gain_own, gain_sib, w_own, w_sib = small_held
    nodes_dev, half_width = agg_own.shape
    width = 2 * half_width
    first_node = idx[1] * nodes_dev
    gsum_own = jnp.zeros((1, half_width), F32)
    gsum_sib = jnp.zeros((1, half_width), F32)

    def row_mean(a, b):
        return jnp.sum(a + b, axis=1, keepdims=True) * (1.0 / width)

    for step in range(steps):
        at = slice(step * rows, (step + 1) * rows)
        column = jnp.transpose(jnp.broadcast_to(recv[:, at], (8, rows)))[:, :1] - first_node
        picks = lax.broadcasted_iota(jnp.int32, (rows, nodes_dev), 1) == column
        picks = jnp.where(picks, 1.0, 0.0).astype(BF16)
        for copy in tiles[step]:
            copy.wait()
        x_own, x_sib, cot_own, cot_sib, hid = (ref[at, :] for ref in tiled_held)
        v_own = x_own.astype(F32)
        v_sib = x_sib.astype(F32)
        mean = row_mean(v_own, v_sib)
        v_own = v_own - mean
        v_sib = v_sib - mean
        inv = lax.rsqrt(row_mean(v_own * v_own, v_sib * v_sib) + 1e-05)
        n_own = v_own * inv
        n_sib = v_sib * inv
        up_own = cot_own.astype(F32) + dot_nn(picks, agg_own[...])
        up_sib = cot_sib.astype(F32) + dot_nn(picks, agg_sib[...])
        wt_own = gain_own[...] * up_own
        wt_sib = gain_sib[...] * up_sib
        mean_first = row_mean(wt_own, wt_sib)
        mean_cross = row_mean(wt_own * n_own, wt_sib * n_sib)
        g_own = (inv * (wt_own - mean_first - n_own * mean_cross)).astype(BF16)
        g_sib = (inv * (wt_sib - mean_first - n_sib * mean_cross)).astype(BF16)
        hidden = dot_nt(g_own, w_own[...]) + dot_nt(g_sib, w_sib[...])
        value = hid.astype(F32)
        sig = 1.0 / (1.0 + jnp.exp(-value))
        act = (value * sig).astype(BF16)
        pre_grad[at, :] = (hidden * (sig * (1.0 + value * (1.0 - sig)))).astype(BF16)
        if step == 0:
            wo_own[...] = dot_tn(g_own, act)
            acc_sib[...] = dot_tn(g_sib, act)
        else:
            wo_own[...] += dot_tn(g_own, act)
            acc_sib[...] += dot_tn(g_sib, act)
        gsum_own = gsum_own + jnp.sum(up_own * n_own, axis=0, keepdims=True)
        gsum_sib = gsum_sib + jnp.sum(up_sib * n_sib, axis=0, keepdims=True)

    gain_out[...] = gsum_own
    small[:half_width, :] = acc_sib[...].astype(BF16)
    small[half_width:, :] = split_rows(gsum_sib, feat_width).astype(BF16)


def pool_kernel(
    shards, steps, idx, g_own, g_sib, edge_lat, send_lat, node_lat, senders, recv, wo_own, gain_own, small, *rest
):
    outs = rest[:shards]
    recv_out, grads, pooled, by_recv = rest[shards:]
    step = pl.program_id(0)
    core, shard = idx[0], idx[1]
    nodes_dev, half_width = node_lat.shape
    half_nodes = nodes_dev // 2
    rows, feat_width = g_own.shape

    @pl.when(step == 0)
    def _():
        grads[...] = jnp.zeros_like(grads)
        pooled[...] = jnp.zeros_like(pooled)
        by_recv[...] = jnp.zeros_like(by_recv)

    grad = jnp.where(step < steps // 2, g_own[...], g_sib[...])
    node_id = lax.broadcasted_iota(jnp.int32, (nodes_dev, rows), 0)
    picks = jnp.where(node_id + shard * nodes_dev == recv[...], 1.0, 0.0).astype(BF16)
    by_recv[...] += dot_nn(picks, grad)
    half_id = lax.broadcasted_iota(jnp.int32, (half_nodes, rows), 0) + core * half_nodes
    for dest in range(shards):
        picks = jnp.where(half_id + dest * nodes_dev == senders[...], 1.0, 0.0).astype(BF16)
        pooled[dest * half_nodes : (dest + 1) * half_nodes, :] += dot_nn(picks, grad)
    grads[:half_width, :] += dot_tn(edge_lat[...], grad)
    grads[half_width : 2 * half_width, :] += dot_tn(send_lat[...], grad)

    @pl.when(step == steps - 1)
    def _():
        sums = by_recv[...]
        high = sums.astype(BF16)
        low = (sums - high.astype(F32)).astype(BF16)
        grads[2 * half_width : 3 * half_width, :] = dot_tn(node_lat[...], high) + dot_tn(node_lat[...], low)
        grads[3 * half_width :, :] = wo_own[...] + small[:half_width, :].astype(F32)
        gain = split_rows(gain_own[...], feat_width) + small[half_width:, :].astype(F32)
        recv_out[...] = high
        block = 4 * half_width // shards
        for k in range(shards):
            dest = lax.rem(shard + k, shards)
            kind = outs[k].dtype
            w_rows = grads[pl.ds(pl.multiple_of(dest * block, 16), block), :]
            outs[k][:block, :] = w_rows.astype(kind)
            outs[k][block : block + PAD, :] = gain.astype(kind)
            s_rows = pooled[pl.ds(pl.multiple_of(dest * half_nodes, 16), half_nodes), :]
            outs[k][block + PAD :, :] = s_rows.astype(kind)


def sum_kernel(shards, *refs):
    w_total, s_total = refs[-2:]
    total = refs[0][...].astype(F32)
    for ref in refs[1:shards]:
        total = total + ref[...].astype(F32)
    rows = w_total.shape[0]
    w_total[...] = total[:rows].astype(BF16)
    s_total[...] = total[rows:].astype(BF16)


def edge_out_kernel(feats, steps, idx, cot, w_edge, *refs):
    own = refs[:feats]
    sib = refs[feats : 2 * feats]
    out, token, held = refs[2 * feats :]
    token[...] = jnp.zeros_like(token)
    step = pl.program_id(0)
    feat_width = own[0].shape[1]
    for k in range(feats):
        source = lax.rem(idx[2] - k + feats, feats)
        piece = jnp.where(step < steps // 2, own[k][...], sib[k][...])
        held[:, pl.ds(pl.multiple_of(source * feat_width, 128), feat_width)] = piece
    out[...] = (cot[...].astype(F32) + dot_nt(held[...], w_edge[...])).astype(BF16)


def finish_kernel(shards, feats, scale, idx, *refs):
    totals = refs[:shards]
    w_send, w_recv = refs[shards : shards + 2]
    by_recv = refs[shards + 2 : shards + 2 + feats]
    sums = refs[shards + 2 + feats : shards + 2 + 3 * feats]
    w_in_grad, w_out_grad, gain_grad, node_grad, held, held_send, held_recv = refs[-7:]
    rows, feat_width = sums[0].shape
    for k in range(feats):
        source = lax.rem(idx[2] - k + feats, feats)
        there = pl.ds(pl.multiple_of(source * feat_width, 128), feat_width)
        held_recv[:, there] = by_recv[k][...]
        for side in range(2):
            at = pl.ds(pl.multiple_of((idx[0] if side == 0 else 1 - idx[0]) * rows, 16), rows)
            held_send[at, there] = sums[2 * k + side][...]
    node_grad[...] = dot_nt(held_send[...], w_send[...]) + dot_nt(held_recv[...], w_recv[...])

    half_width = w_in_grad.shape[1]
    block = 4 * half_width // shards
    for k in range(shards):
        source = lax.rem(idx[1] - k + shards, shards)
        held[pl.ds(pl.multiple_of(source * block, 16), block), :] = totals[k][:block, :].astype(F32) * scale

        @pl.when(source == 0)
        def _(k=k):
            gain = totals[k][block:, :].astype(F32) * scale
            for j in range(half_width // feat_width):
                gain_grad[:, j * feat_width : (j + 1) * feat_width] = gain[j : j + 1, :]

    for k in range(3):
        w_in_grad[k] = held[k * half_width : (k + 1) * half_width, :]
    w_out_grad[...] = jnp.transpose(held[3 * half_width :, :])


def body(
    node_latents, edge_latents, sender_latents, pre_hidden, pre_norm, norm_gain, w_in, w_out, senders, receivers,
    edge_cotangent, agg_cotangent,
):
    shards = lax.axis_size("nodes")
    feats = lax.axis_size("feat")
    core, shard, feat = (lax.axis_index(name) for name in ("chan", "nodes", "feat"))
    idx = jnp.stack([core, shard, feat]).astype(jnp.int32)
    nodes_dev, half_width = node_latents.shape
    edges = edge_latents.shape[0]
    feat_width = pre_hidden.shape[1]
    hidden_width = w_in.shape[2]
    half = edges // 2
    half_nodes = nodes_dev // 2
    scale = 1.0 / math.sqrt(edges * shards)

    def over_chan(x):
        return lax.ppermute(x, "chan", [(0, 1), (1, 0)])

    pre_norm_sib = over_chan(pre_norm)
    cot_sib = over_chan(edge_cotangent)
    agg_sib = over_chan(agg_cotangent)
    w_out_sib = over_chan(w_out)
    gain_own = norm_gain.reshape(1, half_width)
    gain_sib = over_chan(gain_own)
    recv_row = receivers.reshape(1, edges)
    send_row = senders.reshape(1, edges)

    tile = 768
    steps = half // tile
    wide = (tile, half_width)
    narrow = (tile, feat_width)
    smem = pl.BlockSpec(memory_space=pltpu.SMEM)
    vmem = pl.BlockSpec(memory_space=pltpu.VMEM)
    edge_steps = 3
    pre_own, wo_own, gain_sum, small = pl.pallas_call(
        functools.partial(edge_kernel, edge_steps),
        in_specs=[smem] + [pl.BlockSpec(memory_space=pl.ANY)] * 12,
        out_specs=[vmem] * 4,
        out_shape=[
            jax.ShapeDtypeStruct((half, feat_width), BF16),
            jax.ShapeDtypeStruct((half_width, feat_width), F32),
            jax.ShapeDtypeStruct((1, half_width), F32),
            jax.ShapeDtypeStruct((half_width + PAD, feat_width), BF16),
        ],
        scratch_shapes=[
            pltpu.VMEM((1, half), jnp.int32),
            pltpu.VMEM((nodes_dev, half_width), BF16),
            pltpu.VMEM((nodes_dev, half_width), BF16),
            pltpu.VMEM((1, half_width), F32),
            pltpu.VMEM((1, half_width), F32),
            pltpu.VMEM((feat_width, half_width), BF16),
            pltpu.VMEM((feat_width, half_width), BF16),
            pltpu.VMEM((half, half_width), BF16),
            pltpu.VMEM((half, half_width), BF16),
            pltpu.VMEM((half, half_width), BF16),
            pltpu.VMEM((half, half_width), BF16),
            pltpu.VMEM((half, feat_width), BF16),
            pltpu.VMEM((half_width, feat_width), F32),
            pltpu.SemaphoreType.DMA((7,)),
            pltpu.SemaphoreType.DMA((5, edge_steps)),
        ],
        compiler_params=params(),
        cost_estimate=cost(4 * half * (nodes_dev + 2 * feat_width) * half_width, 10 * half * half_width),
        name="edge_norm",
    )(
        idx, in_hbm(recv_row), in_hbm(agg_cotangent), agg_sib, in_hbm(gain_own), gain_sib, in_hbm(w_out), w_out_sib,
        in_hbm(pre_norm), pre_norm_sib, in_hbm(edge_cotangent), cot_sib, in_hbm(pre_hidden),
    )

    pre_sib = over_chan(pre_own)
    small_sib = over_chan(small)
    crossed_own = [pre_own] + [lax.ppermute(pre_own, "feat", ring(feats, k)) for k in range(1, feats)]

    def by_edge(i, s):
        return jnp.where(i < steps, s[0] * steps + i, (1 - s[0]) * steps + i - steps)

    def first_half(i, s):
        return (jnp.minimum(i, steps - 1), 0)

    def second_half(i, s):
        return (jnp.maximum(i - steps, 0), 0)

    block = 4 * half_width // shards
    rows_out = block + PAD + half_nodes
    pool_outs = [jax.ShapeDtypeStruct((rows_out, feat_width), F32 if k == 0 else BF16) for k in range(shards)]
    pool_outs.append(jax.ShapeDtypeStruct((nodes_dev, feat_width), BF16))
    *parts, by_recv = pl.pallas_call(
        functools.partial(pool_kernel, shards, 2 * steps),
        grid_spec=pltpu.PrefetchScalarGridSpec(
            num_scalar_prefetch=1,
            grid=(2 * steps,),
            in_specs=[
                pl.BlockSpec(narrow, first_half),
                pl.BlockSpec(narrow, second_half),
                pl.BlockSpec(wide, lambda i, s: (by_edge(i, s), 0)),
                pl.BlockSpec(wide, lambda i, s: (by_edge(i, s), 0)),
                whole((nodes_dev, half_width)),
                pl.BlockSpec((1, tile), lambda i, s: (0, by_edge(i, s))),
                pl.BlockSpec((1, tile), lambda i, s: (0, by_edge(i, s))),
                whole((half_width, feat_width)),
                whole((1, half_width)),
                whole((half_width + PAD, feat_width)),
            ],
            out_specs=[whole(x.shape) for x in pool_outs],
            scratch_shapes=[
                pltpu.VMEM((4 * half_width, feat_width), F32),
                pltpu.VMEM((shards * half_nodes, feat_width), F32),
                pltpu.VMEM((nodes_dev, feat_width), F32),
            ],
        ),
        out_shape=pool_outs,
        compiler_params=params(),
        cost_estimate=cost(
            2 * edges * feat_width * (nodes_dev + shards * half_nodes + 2 * half_width), 8 * edges * half_width
        ),
        name="pool",
    )(
        idx, pre_own, pre_sib, edge_latents, sender_latents, node_latents, send_row, recv_row, wo_own, gain_sum,
        small_sib,
    )
    arrived = [parts[0]] + [lax.ppermute(parts[k], "nodes", ring(shards, k)) for k in range(1, shards)]
    recv_all = [by_recv] + [lax.ppermute(by_recv, "feat", ring(feats, k)) for k in range(1, feats)]
    w_total, s_total = pl.pallas_call(
        functools.partial(sum_kernel, shards),
        in_specs=[vmem] * shards + [pl.BlockSpec(memory_space=pl.ANY)] * (feats - 1),
        out_shape=[
            jax.ShapeDtypeStruct((block + PAD, feat_width), BF16),
            jax.ShapeDtypeStruct((half_nodes, feat_width), BF16),
        ],
        compiler_params=params(),
        cost_estimate=cost(rows_out * feat_width * shards, 4 * rows_out * feat_width * shards),
        name="sum_parts",
    )(*arrived, *recv_all[1:])
    w_all = [w_total] + [lax.ppermute(w_total, "nodes", ring(shards, k)) for k in range(1, shards)]
    s_all = [s_total, over_chan(s_total)]
    for k in range(1, feats):
        s_all.append(lax.ppermute(s_total, "feat", ring(feats, k)))
        flip = [(2 * f + c, 2 * ((f + k) % feats) + 1 - c) for f in range(feats) for c in range(2)]
        s_all.append(lax.ppermute(s_total, ("feat", "chan"), flip))

    passed, _ = lax.optimization_barrier((crossed_own[1:], s_total))
    crossed_own = [pre_own] + passed
    crossed_sib = [pre_sib] + [over_chan(x) for x in passed]

    edge_grad, edge_token = pl.pallas_call(
        functools.partial(edge_out_kernel, feats, 2 * steps),
        grid_spec=pltpu.PrefetchScalarGridSpec(
            num_scalar_prefetch=1,
            grid=(2 * steps,),
            in_specs=[
                pl.BlockSpec(wide, lambda i, s: (by_edge(i, s), 0)),
                pl.BlockSpec((None, half_width, hidden_width), lambda i, s: (0, 0, 0)),
            ]
            + [pl.BlockSpec(narrow, first_half)] * feats
            + [pl.BlockSpec(narrow, second_half)] * feats,
            out_specs=[pl.BlockSpec(wide, lambda i, s: (by_edge(i, s), 0)), whole((8, 128))],
            scratch_shapes=[pltpu.VMEM((tile, hidden_width), BF16)],
        ),
        out_shape=[jax.ShapeDtypeStruct((edges, half_width), BF16), jax.ShapeDtypeStruct((8, 128), F32)],
        compiler_params=params(),
        cost_estimate=cost(2 * edges * hidden_width * half_width, 8 * edges * half_width),
        name="edge_out",
    )(idx, edge_cotangent, w_in, *crossed_own, *crossed_sib)

    w_in_grad, w_out_grad, gain_grad, node_grad = pl.pallas_call(
        functools.partial(finish_kernel, shards, feats, scale),
        grid=(1,),
        in_specs=[smem]
        + [whole((block + PAD, feat_width))] * shards
        + [
            pl.BlockSpec((None, half_width, hidden_width), lambda *_: (1, 0, 0)),
            pl.BlockSpec((None, half_width, hidden_width), lambda *_: (2, 0, 0)),
        ]
        + [whole((nodes_dev, feat_width))] * feats
        + [whole((half_nodes, feat_width))] * (2 * feats)
        + [pl.BlockSpec(memory_space=pl.ANY)],
        out_specs=[
            whole((3, half_width, feat_width)),
            whole((feat_width, half_width)),
            whole((1, half_width)),
            whole((nodes_dev, half_width)),
        ],
        out_shape=[
            jax.ShapeDtypeStruct((3, half_width, feat_width), F32),
            jax.ShapeDtypeStruct((feat_width, half_width), F32),
            jax.ShapeDtypeStruct((1, half_width), F32),
            jax.ShapeDtypeStruct((nodes_dev, half_width), F32),
        ],
        scratch_shapes=[
            pltpu.VMEM((4 * half_width, feat_width), F32),
            pltpu.VMEM((nodes_dev, hidden_width), BF16),
            pltpu.VMEM((nodes_dev, hidden_width), BF16),
        ],
        compiler_params=params(),
        cost_estimate=cost(4 * nodes_dev * hidden_width * half_width, 8 * nodes_dev * hidden_width),
        name="finish",
    )(idx, *w_all, w_in, w_in, *recv_all, *s_all, edge_token)
    return (node_grad, edge_grad, w_in_grad, w_out_grad, gain_grad.reshape(half_width))


def solution(mesh):
    placed = (
        P(("groups", "nodes"), "chan"),
        P(("groups", "nodes"), "chan"),
        P(("groups", "nodes"), "chan"),
        P(("groups", "nodes"), "feat"),
        P(("groups", "nodes"), "chan"),
        P("chan"),
        P(None, "chan", None),
        P("feat", "chan"),
        P(("groups", "nodes")),
        P(("groups", "nodes")),
        P(("groups", "nodes"), "chan"),
        P(("groups", "nodes"), "chan"),
    )
    return jax.shard_map(
        body,
        mesh=mesh,
        in_specs=placed,
        out_specs=(
            P(("groups", "nodes"), "chan"),
            P(("groups", "nodes"), "chan"),
            P("groups", "chan", "feat"),
            P(("groups", "feat"), "chan"),
            P(("groups", "chan")),
        ),
        check_vma=False,
    )
```

```python
import functools
import math

import jax
import jax.numpy as jnp
from jax import lax
from jax.experimental import pallas as pl
from jax.experimental.pallas import tpu as pltpu
from jax.sharding import PartitionSpec as P

F32 = jnp.float32
BF16 = jnp.bfloat16
PAD = 16


def dot_nn(a, b):
    return lax.dot_general(a, b, (((1,), (0,)), ((), ())), preferred_element_type=F32)


def dot_nt(a, b):
    return lax.dot_general(a, b, (((1,), (1,)), ((), ())), preferred_element_type=F32)


def dot_tn(a, b):
    return lax.dot_general(a, b, (((0,), (0,)), ((), ())), preferred_element_type=F32)


def params(mib=48):
    return pltpu.CompilerParams(vmem_limit_bytes=mib * 1024 * 1024)


def cost(flops, nbytes):
    return pl.CostEstimate(flops=int(flops), bytes_accessed=int(nbytes), transcendentals=0)


def whole(shape):
    return pl.BlockSpec(shape, lambda *_: (0,) * len(shape))


def in_hbm(x):
    return pltpu.with_memory_space_constraint(x, pltpu.HBM)


def ring(size, step):
    return [(i, (i + step) % size) for i in range(size)]


def split_rows(row, width):
    parts = [row[:, j * width : (j + 1) * width] for j in range(row.shape[1] // width)]
    parts.append(jnp.zeros((PAD - len(parts), width), row.dtype))
    return jnp.concatenate(parts, axis=0)


def own_kernel(steps, idx, *refs):
    recv_in, agg_in, cot_in, hid_in, x_in = refs[:5]
    upstream, picked, act_out, slope_out, x_out = refs[5:10]
    recv, agg, cot, hid, sems, x_sem = refs[10:]
    half, feat_width = act_out.shape
    nodes_dev = agg.shape[0]
    rows = half // steps
    first = pl.multiple_of(idx[0] * half, 128)
    copies = [
        pltpu.make_async_copy(recv_in.at[:, pl.ds(first, half)], recv, sems.at[0]),
        pltpu.make_async_copy(agg_in, agg, sems.at[1]),
        pltpu.make_async_copy(hid_in.at[pl.ds(first, half), :], hid, sems.at[2]),
        pltpu.make_async_copy(cot_in.at[pl.ds(first, half), :], cot, sems.at[3]),
    ]
    x_copy = pltpu.make_async_copy(x_in.at[pl.ds(first, half), :], x_out, x_sem)
    for copy in copies:
        copy.start()
    x_copy.start()
    for copy in copies:
        copy.wait()
    for step in range(steps):
        at = slice(step * rows, (step + 1) * rows)
        column = jnp.transpose(jnp.broadcast_to(recv[:, at], (8, rows)))[:, :1] - idx[1] * nodes_dev
        picks = lax.broadcasted_iota(jnp.int32, (rows, nodes_dev), 1) == column
        picks = jnp.where(picks, 1.0, 0.0).astype(BF16)
        picked[at, :] = picks
        upstream[at, :] = cot[at, :].astype(F32) + dot_nn(picks, agg[...])
        value = hid[at, :].astype(F32)
        sig = 1.0 / (1.0 + jnp.exp(-value))
        act_out[at, :] = (value * sig).astype(BF16)
        slope_out[at, :] = sig * (1.0 + value * (1.0 - sig))
    x_copy.wait()


def edge_kernel(steps, idx, *refs):
    upstream, picked, act_in, slope, x_in, gain_own, gain_sib, w_own, w_sib, agg_sib, x_far, cot_far = refs[:12]
    pre_grad, wo_own, gain_out, small = refs[12:16]
    x_held, cot_held, acc_sib, sems = refs[16:]
    half, feat_width = pre_grad.shape
    half_width = x_in.shape[1]
    width = 2 * half_width
    rows = half // steps
    first = pl.multiple_of(idx[0] * half, 128)
    tiles = []
    for step in range(steps):
        here = pl.ds(step * rows, rows)
        there = pl.ds(pl.multiple_of(first + step * rows, 128), rows)
        tiles.append(
            (
                pltpu.make_async_copy(x_far.at[there, :], x_held.at[here, :], sems.at[0, step]),
                pltpu.make_async_copy(cot_far.at[there, :], cot_held.at[here, :], sems.at[1, step]),
            )
        )
    for copies in tiles:
        for copy in copies:
            copy.start()
    gsum_own = jnp.zeros((1, half_width), F32)
    gsum_sib = jnp.zeros((1, half_width), F32)

    def row_mean(a, b):
        return jnp.sum(a + b, axis=1, keepdims=True) * (1.0 / width)

    for step in range(steps):
        at = slice(step * rows, (step + 1) * rows)
        for copy in tiles[step]:
            copy.wait()
        v_own = x_in[at, :].astype(F32)
        v_sib = x_held[at, :].astype(F32)
        mean = row_mean(v_own, v_sib)
        v_own = v_own - mean
        v_sib = v_sib - mean
        inv = lax.rsqrt(row_mean(v_own * v_own, v_sib * v_sib) + 1e-05)
        n_own = v_own * inv
        n_sib = v_sib * inv
        up_own = upstream[at, :]
        up_sib = cot_held[at, :].astype(F32) + dot_nn(picked[at, :], agg_sib[...])
        wt_own = gain_own[...] * up_own
        wt_sib = gain_sib[...] * up_sib
        mean_first = row_mean(wt_own, wt_sib)
        mean_cross = row_mean(wt_own * n_own, wt_sib * n_sib)
        g_own = (inv * (wt_own - mean_first - n_own * mean_cross)).astype(BF16)
        g_sib = (inv * (wt_sib - mean_first - n_sib * mean_cross)).astype(BF16)
        hidden = dot_nt(g_own, w_own[...]) + dot_nt(g_sib, w_sib[...])
        pre_grad[at, :] = (hidden * slope[at, :]).astype(BF16)
        act = act_in[at, :]
        if step == 0:
            wo_own[...] = dot_tn(g_own, act)
            acc_sib[...] = dot_tn(g_sib, act)
        else:
            wo_own[...] += dot_tn(g_own, act)
            acc_sib[...] += dot_tn(g_sib, act)
        gsum_own = gsum_own + jnp.sum(up_own * n_own, axis=0, keepdims=True)
        gsum_sib = gsum_sib + jnp.sum(up_sib * n_sib, axis=0, keepdims=True)

    gain_out[...] = gsum_own
    small[:half_width, :] = acc_sib[...].astype(BF16)
    small[half_width:, :] = split_rows(gsum_sib, feat_width).astype(BF16)


def add_edges(sibling, steps, idx, grad, ins, helds, sems, sums, fresh):
    grads, pooled, by_recv = sums
    core, shard = idx[0], idx[1]
    half, feat_width = grad.shape
    rows = half // steps
    side = 1 - core if sibling else core
    first = pl.multiple_of(side * half, 128)
    copies = []
    for j, (src, dst) in enumerate(zip(ins, helds)):
        src = src.at[:, pl.ds(first, half)] if j < 2 else src.at[pl.ds(first, half), :]
        copies.append(pltpu.make_async_copy(src, dst, sems.at[j]))
    for copy in copies:
        copy.start()
    send_row, recv_row, edge_lat, send_lat = helds
    nodes_dev, half_width = by_recv.shape[0], edge_lat.shape[1]
    half_nodes = nodes_dev // 2

    def put(ref, at, value, step):
        ref[at, :] = value if fresh and step == 0 else ref[at, :] + value

    copies[0].wait()
    copies[1].wait()
    for step in range(steps):
        at = slice(step * rows, (step + 1) * rows)
        node_id = lax.broadcasted_iota(jnp.int32, (nodes_dev, rows), 0) + shard * nodes_dev
        picks = jnp.where(node_id == recv_row[:, at], 1.0, 0.0).astype(BF16)
        put(by_recv, slice(0, nodes_dev), dot_nn(picks, grad[at, :]), step)
        half_id = lax.broadcasted_iota(jnp.int32, (half_nodes, rows), 0) + core * half_nodes
        for dest in range(pooled.shape[0] // half_nodes):
            picks = jnp.where(half_id + dest * nodes_dev == send_row[:, at], 1.0, 0.0).astype(BF16)
            put(pooled, slice(dest * half_nodes, (dest + 1) * half_nodes), dot_nn(picks, grad[at, :]), step)
    copies[2].wait()
    copies[3].wait()
    for step in range(steps):
        at = slice(step * rows, (step + 1) * rows)
        put(grads, slice(0, half_width), dot_tn(edge_lat[at, :], grad[at, :]), step)
        put(grads, slice(half_width, 2 * half_width), dot_tn(send_lat[at, :], grad[at, :]), step)


def pool_own_kernel(steps, idx, grad, *refs):
    add_edges(False, steps, idx, grad, refs[:4], refs[7:11], refs[11], refs[4:7], True)


def pool_kernel(shards, steps, idx, grad, *refs):
    ins, (part_grads, part_pooled, part_recv) = refs[:4], refs[4:7]
    node_lat, wo_own, gain_own, small = refs[7:11]
    outs, recv_out = refs[11 : 11 + shards], refs[11 + shards]
    grads, pooled, by_recv, *helds, sems = refs[12 + shards :]
    shard = idx[1]
    half_width, feat_width = wo_own.shape
    half_nodes = node_lat.shape[0] // 2
    grads[: 2 * half_width, :] = part_grads[...]
    pooled[...] = part_pooled[...]
    by_recv[...] = part_recv[...]
    add_edges(True, steps, idx, grad, ins, helds, sems, (grads, pooled, by_recv), False)
    sums = by_recv[...]
    high = sums.astype(BF16)
    low = (sums - high.astype(F32)).astype(BF16)
    grads[2 * half_width : 3 * half_width, :] = dot_tn(node_lat[...], high) + dot_tn(node_lat[...], low)
    grads[3 * half_width :, :] = wo_own[...] + small[:half_width, :].astype(F32)
    gain = split_rows(gain_own[...], feat_width) + small[half_width:, :].astype(F32)
    recv_out[...] = high
    block = 4 * half_width // shards
    for k in range(shards):
        dest = lax.rem(shard + k, shards)
        kind = outs[k].dtype
        w_rows = grads[pl.ds(pl.multiple_of(dest * block, 16), block), :]
        outs[k][:block, :] = w_rows.astype(kind)
        outs[k][block : block + PAD, :] = gain.astype(kind)
        s_rows = pooled[pl.ds(pl.multiple_of(dest * half_nodes, 16), half_nodes), :]
        outs[k][block + PAD :, :] = s_rows.astype(kind)


def sum_kernel(shards, scale, idx, *refs):
    blocks = refs[:shards]
    w_total, s_total, gain_total, gain_held = refs[-4:]
    total = blocks[0][...].astype(F32)
    for ref in blocks[1:]:
        total = total + ref[...].astype(F32)
    rows = w_total.shape[0]
    w_total[...] = total[:rows].astype(BF16)
    s_total[...] = total[rows + PAD :].astype(BF16)
    for k in range(shards):
        source = lax.rem(idx[1] - k + shards, shards)
        sent = blocks[k][rows : rows + PAD, :].astype(BF16).astype(F32)
        gain_held[pl.ds(pl.multiple_of(source * PAD, PAD), PAD), :] = sent
    gain = gain_held[:PAD, :]
    for k in range(1, shards):
        gain = gain + gain_held[k * PAD : (k + 1) * PAD, :]
    feat_width = gain.shape[1]
    for j in range(gain_total.shape[1] // feat_width):
        gain_total[:, j * feat_width : (j + 1) * feat_width] = gain[j : j + 1, :] * scale


def edge_out_kernel(feats, steps, idx, cot, w_edge, *refs):
    own = refs[:feats]
    sib = refs[feats : 2 * feats]
    out, token, held = refs[2 * feats :]
    token[...] = jnp.zeros_like(token)
    step = pl.program_id(0)
    feat_width = own[0].shape[1]
    for k in range(feats):
        source = lax.rem(idx[2] - k + feats, feats)
        piece = jnp.where(step < steps // 2, own[k][...], sib[k][...])
        held[:, pl.ds(pl.multiple_of(source * feat_width, 128), feat_width)] = piece
    out[...] = (cot[...].astype(F32) + dot_nt(held[...], w_edge[...])).astype(BF16)


def finish_kernel(shards, feats, scale, idx, *refs):
    totals = refs[:1] + refs[1:shards][::-1]
    w_send, w_recv = refs[shards : shards + 2]
    by_recv = refs[shards + 2 : shards + 2 + feats]
    sums = refs[shards + 2 + feats : shards + 2 + 3 * feats][::-1]
    gain_in = refs[shards + 2 + 3 * feats]
    w_in_grad, w_out_grad, gain_grad, node_grad, held, held_send, held_recv = refs[-7:]
    gain_grad[...] = gain_in[...]
    rows, feat_width = sums[0].shape
    for k in range(feats):
        source = lax.rem(idx[2] - k + feats, feats)
        there = pl.ds(pl.multiple_of(source * feat_width, 128), feat_width)
        held_recv[:, there] = by_recv[k][...]
        for side in range(2):
            at = pl.ds(pl.multiple_of((idx[0] if side == 0 else 1 - idx[0]) * rows, 16), rows)
            held_send[at, there] = sums[2 * k + side][...]
    node_grad[...] = dot_nt(held_send[...], w_send[...]) + dot_nt(held_recv[...], w_recv[...])

    half_width = w_in_grad.shape[1]
    block = 4 * half_width // shards
    for k in range(shards):
        source = lax.rem(idx[1] - k + shards, shards)
        held[pl.ds(pl.multiple_of(source * block, 16), block), :] = totals[k][...].astype(F32) * scale

    for k in range(3):
        w_in_grad[k] = held[k * half_width : (k + 1) * half_width, :]
    w_out_grad[...] = jnp.transpose(held[3 * half_width :, :])


def body(
    node_latents, edge_latents, sender_latents, pre_hidden, pre_norm, norm_gain, w_in, w_out, senders, receivers,
    edge_cotangent, agg_cotangent,
):
    shards = lax.axis_size("nodes")
    feats = lax.axis_size("feat")
    core, shard, feat = (lax.axis_index(name) for name in ("chan", "nodes", "feat"))
    idx = jnp.stack([core, shard, feat]).astype(jnp.int32)
    nodes_dev, half_width = node_latents.shape
    edges = edge_latents.shape[0]
    feat_width = pre_hidden.shape[1]
    hidden_width = w_in.shape[2]
    half = edges // 2
    half_nodes = nodes_dev // 2
    scale = 1.0 / math.sqrt(edges * shards)

    def over_chan(x):
        return lax.ppermute(x, "chan", [(0, 1), (1, 0)])

    pre_norm_sib = over_chan(pre_norm)
    cot_sib = over_chan(edge_cotangent)
    agg_sib = over_chan(agg_cotangent)
    w_out_sib = over_chan(w_out)
    gain_own = norm_gain.reshape(1, half_width)
    gain_sib = over_chan(gain_own)
    recv_row = receivers.reshape(1, edges)
    send_row = senders.reshape(1, edges)

    tile = 768
    steps = half // tile
    wide = (tile, half_width)
    narrow = (tile, feat_width)
    smem = pl.BlockSpec(memory_space=pltpu.SMEM)
    vmem = pl.BlockSpec(memory_space=pltpu.VMEM)
    edge_steps = 3
    any_space = pl.BlockSpec(memory_space=pl.ANY)
    upstream, picked, act, slope, x_near = pl.pallas_call(
        functools.partial(own_kernel, edge_steps),
        in_specs=[smem] + [any_space] * 5,
        out_specs=[vmem] * 5,
        out_shape=[
            jax.ShapeDtypeStruct((half, half_width), F32),
            jax.ShapeDtypeStruct((half, nodes_dev), BF16),
            jax.ShapeDtypeStruct((half, feat_width), BF16),
            jax.ShapeDtypeStruct((half, feat_width), F32),
            jax.ShapeDtypeStruct((half, half_width), BF16),
        ],
        scratch_shapes=[
            pltpu.VMEM((1, half), jnp.int32),
            pltpu.VMEM((nodes_dev, half_width), BF16),
            pltpu.VMEM((half, half_width), BF16),
            pltpu.VMEM((half, feat_width), BF16),
            pltpu.SemaphoreType.DMA((4,)),
            pltpu.SemaphoreType.DMA,
        ],
        compiler_params=params(24),
        cost_estimate=cost(2 * half * nodes_dev * half_width, 8 * half * half_width),
        name="own_edges",
    )(idx, *(in_hbm(x) for x in (recv_row, agg_cotangent, edge_cotangent, pre_hidden, pre_norm)))
    pre_own, wo_own, gain_sum, small = pl.pallas_call(
        functools.partial(edge_kernel, edge_steps),
        in_specs=[smem] + [vmem] * 10 + [any_space] * 2,
        out_specs=[vmem] * 4,
        out_shape=[
            jax.ShapeDtypeStruct((half, feat_width), BF16),
            jax.ShapeDtypeStruct((half_width, feat_width), F32),
            jax.ShapeDtypeStruct((1, half_width), F32),
            jax.ShapeDtypeStruct((half_width + PAD, feat_width), BF16),
        ],
        scratch_shapes=[
            pltpu.VMEM((half, half_width), BF16),
            pltpu.VMEM((half, half_width), BF16),
            pltpu.VMEM((half_width, feat_width), F32),
            pltpu.SemaphoreType.DMA((2, edge_steps)),
        ],
        compiler_params=params(32),
        cost_estimate=cost(4 * half * (nodes_dev + 2 * feat_width) * half_width, 10 * half * half_width),
        name="edge_norm",
    )(
        idx, upstream, picked, act, slope, x_near, gain_own, gain_sib, w_out, w_out_sib, agg_sib, pre_norm_sib,
        cot_sib,
    )

    pre_sib = over_chan(pre_own)
    small_sib = over_chan(small)

    def by_edge(i, s):
        return jnp.where(i < steps, s[0] * steps + i, (1 - s[0]) * steps + i - steps)

    def first_half(i, s):
        return (jnp.minimum(i, steps - 1), 0)

    def second_half(i, s):
        return (jnp.maximum(i - steps, 0), 0)

    block = 4 * half_width // shards
    rows_out = block + PAD + half_nodes
    pool_outs = [jax.ShapeDtypeStruct((rows_out, feat_width), F32 if k == 0 else BF16) for k in range(shards)]
    pool_outs.append(jax.ShapeDtypeStruct((nodes_dev, feat_width), BF16))
    pool_steps = 1
    sum_shapes = [
        jax.ShapeDtypeStruct((rows, feat_width), F32) for rows in (2 * half_width, shards * half_nodes, nodes_dev)
    ]
    held_shapes = [
        pltpu.VMEM((1, half), jnp.int32),
        pltpu.VMEM((1, half), jnp.int32),
        pltpu.VMEM((half, half_width), BF16),
        pltpu.VMEM((half, half_width), BF16),
        pltpu.SemaphoreType.DMA((4,)),
    ]
    pool_cost = cost(
        edges * feat_width * (nodes_dev + shards * half_nodes + 2 * half_width), 4 * edges * half_width
    )
    by_edge_args = [in_hbm(x) for x in (send_row, recv_row, edge_latents, sender_latents)]
    any_space = pl.BlockSpec(memory_space=pl.ANY)
    part_sums = pl.pallas_call(
        functools.partial(pool_own_kernel, pool_steps),
        in_specs=[smem, vmem] + [any_space] * 4,
        out_specs=[vmem] * 3,
        out_shape=sum_shapes,
        scratch_shapes=held_shapes,
        compiler_params=params(),
        cost_estimate=pool_cost,
        name="pool_own",
    )(idx, pre_own, *by_edge_args)
    *parts, by_recv = pl.pallas_call(
        functools.partial(pool_kernel, shards, pool_steps),
        in_specs=[smem, vmem] + [any_space] * 4 + [vmem] * 7,
        out_specs=[vmem] * (shards + 1),
        out_shape=pool_outs,
        scratch_shapes=[
            pltpu.VMEM((4 * half_width, feat_width), F32),
            pltpu.VMEM((shards * half_nodes, feat_width), F32),
            pltpu.VMEM((nodes_dev, feat_width), F32),
        ]
        + held_shapes,
        compiler_params=params(),
        cost_estimate=pool_cost,
        name="pool",
    )(idx, pre_sib, *by_edge_args, *part_sums, node_latents, wo_own, gain_sum, small_sib)
    pre_sent, by_recv = lax.optimization_barrier((pre_own, by_recv))
    crossed_own = [pre_own] + [lax.ppermute(pre_sent, "feat", ring(feats, k)) for k in range(1, feats)]
    arrived = [parts[0]] + [lax.ppermute(parts[k], "nodes", ring(shards, k)) for k in range(1, shards)]
    recv_all = [by_recv] + [lax.ppermute(by_recv, "feat", ring(feats, k)) for k in range(1, feats)]
    w_total, s_total, gain_sum = pl.pallas_call(
        functools.partial(sum_kernel, shards, scale),
        in_specs=[smem] + [vmem] * shards + [any_space] * (feats - 1),
        out_shape=[
            jax.ShapeDtypeStruct((block, feat_width), BF16),
            jax.ShapeDtypeStruct((half_nodes, feat_width), BF16),
            jax.ShapeDtypeStruct((1, half_width), F32),
        ],
        scratch_shapes=[pltpu.VMEM((shards * PAD, feat_width), F32)],
        compiler_params=params(),
        cost_estimate=cost(rows_out * feat_width * shards, 4 * rows_out * feat_width * shards),
        name="sum_parts",
    )(idx, *arrived, *recv_all[1:])
    w_all = [w_total] + [lax.ppermute(w_total, "nodes", ring(shards, k)) for k in range(1, shards)]
    s_all = [s_total, over_chan(s_total)]
    for k in range(1, feats):
        s_all.append(lax.ppermute(s_total, "feat", ring(feats, k)))
        flip = [(2 * f + c, 2 * ((f + k) % feats) + 1 - c) for f in range(feats) for c in range(2)]
        s_all.append(lax.ppermute(s_total, ("feat", "chan"), flip))

    passed, _ = lax.optimization_barrier((crossed_own[1:], s_total))
    crossed_own = [pre_own] + passed
    crossed_sib = [pre_sib] + [over_chan(x) for x in passed]

    edge_grad, edge_token = pl.pallas_call(
        functools.partial(edge_out_kernel, feats, 2 * steps),
        grid_spec=pltpu.PrefetchScalarGridSpec(
            num_scalar_prefetch=1,
            grid=(2 * steps,),
            in_specs=[
                pl.BlockSpec(wide, lambda i, s: (by_edge(i, s), 0)),
                pl.BlockSpec((None, half_width, hidden_width), lambda i, s: (0, 0, 0)),
            ]
            + [pl.BlockSpec(narrow, first_half)] * feats
            + [pl.BlockSpec(narrow, second_half)] * feats,
            out_specs=[pl.BlockSpec(wide, lambda i, s: (by_edge(i, s), 0)), whole((8, 128))],
            scratch_shapes=[pltpu.VMEM((tile, hidden_width), BF16)],
        ),
        out_shape=[jax.ShapeDtypeStruct((edges, half_width), BF16), jax.ShapeDtypeStruct((8, 128), F32)],
        compiler_params=params(),
        cost_estimate=cost(2 * edges * hidden_width * half_width, 8 * edges * half_width),
        name="edge_out",
    )(idx, edge_cotangent, w_in, *crossed_own, *crossed_sib)

    w_in_grad, w_out_grad, gain_grad, node_grad = pl.pallas_call(
        functools.partial(finish_kernel, shards, feats, scale),
        grid=(1,),
        in_specs=[smem]
        + [whole((block, feat_width))] * shards
        + [
            pl.BlockSpec((None, half_width, hidden_width), lambda *_: (1, 0, 0)),
            pl.BlockSpec((None, half_width, hidden_width), lambda *_: (2, 0, 0)),
        ]
        + [whole((nodes_dev, feat_width))] * feats
        + [whole((half_nodes, feat_width))] * (2 * feats)
        + [whole((1, half_width))]
        + [pl.BlockSpec(memory_space=pl.ANY)],
        out_specs=[
            whole((3, half_width, feat_width)),
            whole((feat_width, half_width)),
            whole((1, half_width)),
            whole((nodes_dev, half_width)),
        ],
        out_shape=[
            jax.ShapeDtypeStruct((3, half_width, feat_width), F32),
            jax.ShapeDtypeStruct((feat_width, half_width), F32),
            jax.ShapeDtypeStruct((1, half_width), F32),
            jax.ShapeDtypeStruct((nodes_dev, half_width), F32),
        ],
        scratch_shapes=[
            pltpu.VMEM((4 * half_width, feat_width), F32),
            pltpu.VMEM((nodes_dev, hidden_width), BF16),
            pltpu.VMEM((nodes_dev, hidden_width), BF16),
        ],
        compiler_params=params(),
        cost_estimate=cost(4 * nodes_dev * hidden_width * half_width, 8 * nodes_dev * hidden_width),
        name="finish",
    )(idx, w_total, *w_all[:0:-1], w_in, w_in, *recv_all, *s_all[::-1], gain_sum, edge_token)
    return (node_grad, edge_grad, w_in_grad, w_out_grad, gain_grad.reshape(half_width))


def solution(mesh):
    placed = (
        P(("groups", "nodes"), "chan"),
        P(("groups", "nodes"), "chan"),
        P(("groups", "nodes"), "chan"),
        P(("groups", "nodes"), "feat"),
        P(("groups", "nodes"), "chan"),
        P("chan"),
        P(None, "chan", None),
        P("feat", "chan"),
        P(("groups", "nodes")),
        P(("groups", "nodes")),
        P(("groups", "nodes"), "chan"),
        P(("groups", "nodes"), "chan"),
    )
    return jax.shard_map(
        body,
        mesh=mesh,
        in_specs=placed,
        out_specs=(
            P(("groups", "nodes"), "chan"),
            P(("groups", "nodes"), "chan"),
            P("groups", "chan", "feat"),
            P(("groups", "feat"), "chan"),
            P(("groups", "chan")),
        ),
        check_vma=False,
    )
```
